32 devices in a mesh: row: 8 (over z, x), col: 4 (over y, core).
Axes of the slice: x: 2, y: 2, z: 4, core: 2. Of those that a mesh axis runs over, the one named last changes fastest.
Arguments:
- strips: bfloat16 [160, 8, 4, 64, 512], P('col', 'row'), may hold values from -6 to 6
- pair_counts: int32 [160, 8, 2], P('col', 'row'), may hold values from 0 to 5, as said below
- pair_offsets: int32 [160, 8, 2], P('col', 'row'), may hold values from 0 to 63
- tile_stiffness: float32 [160, 8], P('col', 'row'), may hold values from 0.1 to 1
- anchor: float32 [160, 8, 896], P('col', 'row'), may hold values from 0.02 to 0.2
Outputs:
- match_terms: float32 [160, 8, 2, 3, 8], P('col', 'row')
- positions: float32 [160, 8, 2, 896], P('col', 'row')
- residual: float32 [160, 8, 2, 896], P('col', 'row')
The draws below stay inside these ranges and needn't reach their ends.
Inputs may be any that keep to these rules, and one draw needn't show every extreme that they name: `pair_counts`: entry [r, c, 0] belongs to the pair of tiles (r, c) and (r, c + 1), entry [r, c, 1] to tiles (r, c) and (r + 1, c); it is 0 where the second tile does not exist. The 40 tiles of one device (40 consecutive tile rows of one tile column) hold at most 400 valid blocks in all, and some device holds exactly 400.
All inputs are finite; a program needn't handle non-finite values.
Results may differ from the reference program's by a relative error of at most 0.0082.
Values may be sent and summed in bfloat16 or wider, within the bound.
A program may use at most 128 MiB of HBM per device.

```python
import math
import jax
import jax.numpy as jnp
from jax import lax

TR_DEV = 40
PATCH = 64
BLOCKS = 8
MESH_Y = 28
MESH_X = 32
MATCH_MOST = 5
ITERS = 3
TILE_ROWS = 160
TILE_COLS = 8
NODES = 896


def draw_pair_counts(key, part):
    level_key, raw_key, row_key, col_key = jax.random.split(jax.random.fold_in(key, 17), 4)
    device_rows = TILE_ROWS // TR_DEV
    levels = jax.random.randint(level_key, (device_rows, TILE_COLS), 1, MATCH_MOST + 1)
    tile_levels = jnp.repeat(levels, TR_DEV, axis=0)
    raw_counts = jax.random.randint(raw_key, (TILE_ROWS, TILE_COLS, 2), 0, MATCH_MOST + 1)
    counts = jnp.minimum(raw_counts, tile_levels[:, :, None])
    busy_row = jax.random.randint(row_key, (), 0, device_rows - 1)
    busy_col = jax.random.randint(col_key, (), 0, TILE_COLS - 1)
    tile_row = jnp.arange(TILE_ROWS, dtype=jnp.int32)[:, None]
    col_index = jnp.arange(TILE_COLS, dtype=jnp.int32)[None, :]
    busy_tiles = (tile_row // TR_DEV == busy_row) & (col_index == busy_col)
    counts = jnp.where(busy_tiles[:, :, None], MATCH_MOST, counts)
    east_counts = jnp.where(col_index == TILE_COLS - 1, 0, counts[:, :, 0])
    south_counts = jnp.where(tile_row == TILE_ROWS - 1, 0, counts[:, :, 1])
    return jnp.stack([east_counts, south_counts], axis=2).astype(jnp.int32)


def touch_ends(array, rng, low, top_value):
    longest = array.shape.index(max(array.shape))
    spots = []
    for shift in (0, 1):
        where = [jax.random.randint(jax.random.fold_in(rng, axis), (), 0, length) for axis, length in enumerate(array.shape)]
        where[longest] = (where[longest] + shift) % array.shape[longest]
        spots.append(tuple(where))
    return array.at[spots[0]].set(low).at[spots[1]].set(top_value)


def block_levels(own_key, extent, pieces, least, high):
    level, own = 1.0, jax.random.fold_in(own_key, 6)
    for axis_at, parts in pieces:
        heights = jnp.exp(jax.random.uniform(jax.random.fold_in(own, axis_at), (parts,), jnp.float32, least / len(pieces), high / len(pieces)))
        level = level * jnp.repeat(heights, extent[axis_at] // parts).reshape([-1 if axis == axis_at else 1 for axis in range(len(extent))])
    return level


def noise(stream_key, dims, scale, most, cuts=(), kind=jnp.bfloat16):
    loudness = block_levels(stream_key, dims, cuts, -0.22, 0.18) if cuts else 1.0
    entries = jax.random.normal(stream_key, dims, jnp.float32) * scale * loudness
    return jnp.minimum(jnp.maximum(entries, -most), most).astype(kind)


def setup_inputs(seed: int = 0) -> dict:
    key_of = jax.random.split(jax.random.key(seed), 6)
    return {
        "strips": noise(key_of[0], (TILE_ROWS, TILE_COLS, 4, PATCH, PATCH * BLOCKS), 1.0, 6.0, ((0, 4), (1, 8))),
        "pair_counts": draw_pair_counts(jax.random.fold_in(key_of[5], 71), 0),
        "pair_offsets": touch_ends(jax.random.randint(key_of[2], (TILE_ROWS, TILE_COLS, 2), 0, 64), jax.random.fold_in(key_of[2], 1), 0, 63).astype(jnp.int32),
        "tile_stiffness": jnp.clip(jnp.exp(math.log(1.0) - 2.3025851 * jax.random.uniform(key_of[3], (TILE_ROWS, TILE_COLS), jnp.float32) ** block_levels(key_of[3], (TILE_ROWS, TILE_COLS), ((0, 4), (1, 8)), -0.2, 0.2)), 0.1, 1.0),
        "anchor": jnp.clip(jnp.exp(math.log(0.2) - 2.3025851 * jax.random.uniform(key_of[4], (TILE_ROWS, TILE_COLS, NODES), jnp.float32) ** block_levels(key_of[4], (TILE_ROWS, TILE_COLS, NODES), ((0, 4), (1, 8)), -0.2, 0.2)), 0.02, 0.2),
    }


SMALL_WEIGHT = 1e-6
NODE_GAP = 16.0
HIGHEST_PREC = lax.Precision.HIGHEST


def dft_tables(patch_len):
    index_line = jnp.arange(patch_len, dtype=jnp.int32)
    product = (index_line[:, None] * index_line[None, :]) % patch_len
    angles = product.astype(jnp.float32) * (2.0 * math.pi / patch_len)
    return jnp.cos(angles).astype(jnp.bfloat16), jnp.sin(angles).astype(jnp.bfloat16)


def spectrum(patches, cosine, sine_table):
    patch_len = cosine.shape[0]
    depth_table = jnp.concatenate([cosine, -sine_table], axis=0).astype(jnp.float32)
    length_table = jnp.concatenate([cosine, sine_table], axis=1).astype(jnp.float32)
    half_spec = jnp.einsum("fd,ndbk->nfbk", depth_table, patches.astype(jnp.float32), precision=HIGHEST_PREC)
    half_spec = half_spec.astype(jnp.bfloat16)
    full_spec = jnp.einsum("nfbk,kg->nfbg", half_spec.astype(jnp.float32), length_table, precision=HIGHEST_PREC)
    real_part = full_spec[:, :patch_len, :, :patch_len] + full_spec[:, patch_len:, :, patch_len:]
    imag_part = full_spec[:, patch_len:, :, :patch_len] - full_spec[:, :patch_len, :, patch_len:]
    return real_part, imag_part


def correlate(first_blocks, second_blocks, cosine, sine_table):
    patch_len = cosine.shape[0]
    first_real, first_imag = spectrum(first_blocks, cosine, sine_table)
    second_real, second_imag = spectrum(second_blocks, cosine, sine_table)
    denominator = 0.5 * (first_real * first_real + first_imag * first_imag
                         + second_real * second_real + second_imag * second_imag) + 1.0
    cross_real = ((first_real * second_real + first_imag * second_imag) / denominator).astype(jnp.bfloat16)
    cross_imag = ((first_imag * second_real - first_real * second_imag) / denominator).astype(jnp.bfloat16)
    cross_stack = jnp.concatenate([cross_real, cross_imag], axis=1).astype(jnp.float32)
    length_table = jnp.concatenate([cosine, sine_table], axis=1).astype(jnp.float32)
    back_spec = jnp.einsum("nubv,vg->nubg", cross_stack, length_table, precision=HIGHEST_PREC)
    inverse_real = back_spec[:, :patch_len, :, :patch_len] - back_spec[:, patch_len:, :, patch_len:]
    inverse_imag = back_spec[:, patch_len:, :, :patch_len] + back_spec[:, :patch_len, :, patch_len:]
    half_back = jnp.concatenate([inverse_real, inverse_imag], axis=1).astype(jnp.bfloat16)
    back_table = jnp.concatenate([cosine, -sine_table], axis=1).astype(jnp.float32)
    surface = jnp.einsum("xu,nubv->nxbv", back_table, half_back.astype(jnp.float32), precision=HIGHEST_PREC)
    surface = surface / float(patch_len * patch_len)
    power_map = surface * surface
    offsets = ((jnp.arange(patch_len, dtype=jnp.int32) + patch_len // 2) % patch_len - patch_len // 2).astype(jnp.float32)
    weight = jnp.sum(power_map, axis=(1, 3))
    weight_total = weight + SMALL_WEIGHT
    shift_depth = jnp.sum(power_map * offsets[None, :, None, None], axis=(1, 3)) / weight_total
    shift_along = jnp.sum(power_map * offsets[None, None, None, :], axis=(1, 3)) / weight_total
    return weight, shift_depth, shift_along


def edge_tents(offsets, node_count, blocks, patch_len):
    centres = offsets[..., None] + (patch_len * jnp.arange(blocks, dtype=jnp.int32) + patch_len // 2).astype(offsets.dtype)
    node_pos = (NODE_GAP * jnp.arange(node_count, dtype=jnp.int32).astype(offsets.dtype) + NODE_GAP / 2)
    return jnp.maximum(0.0, 1.0 - jnp.abs(centres[..., None] - node_pos) / NODE_GAP)


def spread(tent_table, weight, vectors):
    return jnp.einsum("...kn,...ck->...cn", tent_table * weight[..., None], vectors, precision=HIGHEST_PREC)


def edge_force(tent_table, weight, difference):
    projected = jnp.einsum("...kn,...cn->...ck", tent_table, difference, precision=HIGHEST_PREC)
    return spread(tent_table, weight, projected)


def intra_term(mesh_grid, stiffness, anchor_grid):
    count_y, count_x = mesh_grid.shape[-2], mesh_grid.shape[-1]
    widths = [(0, 0)] * (mesh_grid.ndim - 2) + [(1, 1), (1, 1)]
    padded = jnp.pad(mesh_grid, widths)
    beside = padded[..., :-2, 1:-1] + padded[..., 2:, 1:-1] + padded[..., 1:-1, :-2] + padded[..., 1:-1, 2:]
    row_ids = jnp.arange(count_y, dtype=jnp.int32)[:, None]
    col_ids = jnp.arange(count_x, dtype=jnp.int32)[None, :]
    degree = ((row_ids > 0).astype(mesh_grid.dtype) + (row_ids < count_y - 1).astype(mesh_grid.dtype)
              + (col_ids > 0).astype(mesh_grid.dtype) + (col_ids < count_x - 1).astype(mesh_grid.dtype))
    return stiffness * (degree * mesh_grid - beside) + anchor_grid * mesh_grid


def place_pairs(result, east_force, south_force):
    result = result.at[..., :, MESH_X - 1].add(east_force)
    pushed_east = jnp.concatenate([jnp.zeros_like(east_force[:, :1]), east_force[:, :-1]], axis=1)
    result = result.at[..., :, 0].add(-pushed_east)
    result = result.at[..., MESH_Y - 1, :].add(south_force)
    pushed_south = jnp.concatenate([jnp.zeros_like(south_force[:1]), south_force[:-1]], axis=0)
    result = result.at[..., 0, :].add(-pushed_south)
    return result


def operate(node_field, stiffness, anchor_grid, east_pair, south_pair):
    tile_rows, tile_cols = node_field.shape[0], node_field.shape[1]
    mesh_grid = node_field.reshape(tile_rows, tile_cols, 2, MESH_Y, MESH_X)
    result = intra_term(mesh_grid, stiffness, anchor_grid)
    right_col = mesh_grid[..., :, MESH_X - 1]
    left_col = mesh_grid[..., :, 0]
    partner_left = jnp.concatenate([left_col[:, 1:], jnp.zeros_like(left_col[:, :1])], axis=1)
    east_force = edge_force(east_pair[0], east_pair[1], right_col - partner_left)
    bottom_row = mesh_grid[..., MESH_Y - 1, :]
    top_row = mesh_grid[..., 0, :]
    partner_top = jnp.concatenate([top_row[1:], jnp.zeros_like(top_row[:1])], axis=0)
    south_force = edge_force(south_pair[0], south_pair[1], bottom_row - partner_top)
    result = place_pairs(result, east_force, south_force)
    return result.reshape(tile_rows, tile_cols, 2, MESH_Y * MESH_X)


def reference(strips, pair_counts, pair_offsets, tile_stiffness, anchor):
    tile_rows, tile_cols = strips.shape[0], strips.shape[1]
    patch_len = strips.shape[3]
    blocks = strips.shape[4] // patch_len
    cosine, sine_table = dft_tables(patch_len)

    def row_terms(row_index):
        here_row = lax.dynamic_index_in_dim(strips, row_index, 0, keepdims=False)
        below_row = lax.dynamic_index_in_dim(strips, jnp.minimum(row_index + 1, tile_rows - 1), 0, keepdims=False)
        east_left = jnp.concatenate([here_row[1:, 0], here_row[-1:, 0]], axis=0)
        first_blocks = jnp.concatenate([here_row[:, 3], here_row[:, 2]], axis=0)
        second_blocks = jnp.concatenate([east_left, below_row[:, 1]], axis=0)
        first_blocks = first_blocks.reshape(2 * tile_cols, patch_len, blocks, patch_len)
        second_blocks = second_blocks.reshape(2 * tile_cols, patch_len, blocks, patch_len)
        return correlate(first_blocks, second_blocks, cosine, sine_table)

    row_list = jnp.arange(tile_rows, dtype=jnp.int32)
    weight, shift_depth, shift_along = lax.map(row_terms, row_list)

    def by_tile(values):
        return values.reshape(tile_rows, 2, tile_cols, blocks).transpose(0, 2, 1, 3)

    is_valid = jnp.arange(blocks, dtype=jnp.int32)[None, None, None, :] < pair_counts[..., None]
    weight = jnp.where(is_valid, by_tile(weight), 0.0)
    shift_depth = jnp.where(is_valid, by_tile(shift_depth), 0.0)
    shift_along = jnp.where(is_valid, by_tile(shift_along), 0.0)
    shift_x = jnp.stack([shift_depth[:, :, 0], shift_along[:, :, 1]], axis=2)
    shift_y = jnp.stack([shift_along[:, :, 0], shift_depth[:, :, 1]], axis=2)
    match_terms = jnp.stack([weight, shift_x, shift_y], axis=3)

    offsets = pair_offsets.astype(jnp.float32)
    east_tent = edge_tents(offsets[:, :, 0], MESH_Y, blocks, patch_len)
    south_tent = edge_tents(offsets[:, :, 1], MESH_X, blocks, patch_len)
    east_pair = (east_tent, weight[:, :, 0])
    south_pair = (south_tent, weight[:, :, 1])
    east_shift = jnp.stack([shift_x[:, :, 0], shift_y[:, :, 0]], axis=2)
    south_shift = jnp.stack([shift_x[:, :, 1], shift_y[:, :, 1]], axis=2)
    zero_grid = jnp.zeros((tile_rows, tile_cols, 2, MESH_Y, MESH_X), jnp.float32)
    rhs_grid = place_pairs(zero_grid, spread(east_tent, weight[:, :, 0], east_shift),
                           spread(south_tent, weight[:, :, 1], south_shift))
    right_side = rhs_grid.reshape(tile_rows, tile_cols, 2, MESH_Y * MESH_X)

    stiffness = tile_stiffness[:, :, None, None, None]
    anchor_grid = anchor.reshape(tile_rows, tile_cols, 1, MESH_Y, MESH_X)
    positions = jnp.zeros_like(right_side)
    residual = right_side
    direction = right_side
    norm_now = jnp.sum(residual * residual)
    for iteration in range(ITERS):
        applied = operate(direction, stiffness, anchor_grid, east_pair, south_pair)
        step_size = norm_now / jnp.sum(direction * applied)
        positions = positions + step_size * direction
        residual = residual - step_size * applied
        norm_next = jnp.sum(residual * residual)
        direction = residual + (norm_next / norm_now) * direction
        norm_now = norm_next
    return match_terms, positions, residual
```

```python
import math

import jax
import jax.numpy as jnp
import numpy as np
from jax import lax
from jax.experimental import pallas as pl
from jax.experimental.pallas import tpu as pltpu
from jax.sharding import PartitionSpec as P

MESH_Y = 28
MESH_X = 32
PATCH = 64
MOST = 5
GROUP = 4
WIDE = 384
PACKED = 2 * MOST * PATCH
SMALL_WEIGHT = 1e-06
NODE_GAP = 16.0
HIGHEST_PREC = lax.Precision.HIGHEST


def tables():
    line = np.arange(PATCH)
    angles = (line[:, None] * line[None, :] % PATCH) * (2.0 * math.pi / PATCH)
    cosine, sine = np.cos(angles), np.sin(angles)
    two = np.eye(2)
    cos2, sin2 = np.kron(two, cosine), np.kron(two, sine)
    depth = np.concatenate([cosine, -sine], axis=0)
    length = np.block([[cos2, -sin2], [sin2, cos2]])
    back_length = np.block([[cos2, sin2], [-sin2, cos2]])
    back_depth = np.concatenate([cosine, -sine], axis=1)
    return [jnp.asarray(t, jnp.bfloat16) for t in (depth, length, back_length, back_depth)]


def pack_two(a, b):
    tail = jnp.concatenate([a[:, 256:320], b[:, 256:320]], axis=1)
    return jnp.concatenate([a[:, :256], b[:, :256], tail], axis=1)


def block_sums(first, second, depth_ref, length_ref, back_length_ref, back_depth_ref):
    count = first.shape[1] // 128
    depth_table = depth_ref[...]

    def by_rows(strip):
        half = jnp.dot(depth_table, strip, preferred_element_type=jnp.float32).astype(jnp.bfloat16)
        return [
            jnp.concatenate([half[:64, 128 * j : 128 * j + 128], half[64:, 128 * j : 128 * j + 128]], axis=1)
            for j in range(count)
        ]

    rows = jnp.concatenate(by_rows(first) + by_rows(second), axis=0)
    spec = jnp.dot(rows, length_ref[...], preferred_element_type=jnp.float32)
    half_rows = 64 * count
    ar, ai = spec[:half_rows, :128], spec[:half_rows, 128:]
    br, bi = spec[half_rows:, :128], spec[half_rows:, 128:]
    inverse = 1.0 / (0.5 * (ar * ar + ai * ai + br * br + bi * bi) + 1.0)
    cross_real = ((ar * br + ai * bi) * inverse).astype(jnp.bfloat16)
    cross_imag = ((ai * br - ar * bi) * inverse).astype(jnp.bfloat16)
    cross = jnp.concatenate([cross_real, cross_imag], axis=1)
    back = jnp.dot(cross, back_length_ref[...], preferred_element_type=jnp.float32).astype(jnp.bfloat16)
    columns = jnp.concatenate(
        [
            jnp.concatenate([back[64 * j : 64 * j + 64, :128], back[64 * j : 64 * j + 64, 128:]], axis=0)
            for j in range(count)
        ],
        axis=1,
    )
    surface = jnp.dot(back_depth_ref[...], columns, preferred_element_type=jnp.float32)
    power = surface * surface
    row_id = lax.broadcasted_iota(jnp.int32, (64, 1), 0)
    depth_offset = ((row_id + 32) % 64 - 32).astype(jnp.float32)
    plain = jnp.sum(power, axis=0, keepdims=True)
    deep = jnp.sum(power * depth_offset, axis=0, keepdims=True)
    plain = jnp.concatenate([plain[:, 128 * j : 128 * j + 128] for j in range(count)], axis=0)
    deep = jnp.concatenate([deep[:, 128 * j : 128 * j + 128] for j in range(count)], axis=0)
    lane = lax.broadcasted_iota(jnp.int32, (count, 128), 1)
    along = plain * ((lane % 64 + 32) % 64 - 32).astype(jnp.float32)
    low = lane < 64
    out = jnp.zeros((count, 128), jnp.float32)
    scale = 1.0 / float(PATCH**4)
    for k, value in enumerate((plain, deep, along)):
        even = jnp.sum(jnp.where(low, value, 0.0), axis=1, keepdims=True) * scale
        odd = jnp.sum(jnp.where(low, 0.0, value), axis=1, keepdims=True) * scale
        out = jnp.where(lane == 2 * k, even, out)
        out = jnp.where(lane == 2 * k + 1, odd, out)
    return out


def south_kernel(first_ref, top_ref, below_ref, next_ref, d_ref, l_ref, bl_ref, bd_ref, out_ref):
    last = pl.program_id(0) == pl.num_programs(0) - 1
    lower = jnp.where(last, next_ref[0], below_ref[0])
    first = jnp.concatenate([pack_two(first_ref[0], first_ref[1]), pack_two(first_ref[2], first_ref[3])], axis=1)
    second = jnp.concatenate([pack_two(top_ref[1], top_ref[2]), pack_two(top_ref[3], lower)], axis=1)
    out_ref[0] = block_sums(first, second, d_ref, l_ref, bl_ref, bd_ref)


def east_kernel(first_ref, second_ref, d_ref, l_ref, bl_ref, bd_ref, out_ref):
    first = jnp.concatenate([pack_two(first_ref[0], first_ref[1]), pack_two(first_ref[2], first_ref[3])], axis=1)
    second = jnp.concatenate([second_ref[0], second_ref[1]], axis=1)
    out_ref[0] = block_sums(first, second, d_ref, l_ref, bl_ref, bd_ref)


def pack_kernel(left_ref, out_ref):
    out_ref[0] = pack_two(left_ref[0], left_ref[1])
    out_ref[1] = pack_two(left_ref[2], left_ref[3])


def strip_spec(side, start=0):
    return pl.BlockSpec((GROUP, None, None, PATCH, WIDE), lambda i: (i + start, 0, side, 0, 0))


def table_specs():
    return [
        pl.BlockSpec((128, 64), lambda i: (0, 0)),
        pl.BlockSpec((256, 256), lambda i: (0, 0)),
        pl.BlockSpec((256, 256), lambda i: (0, 0)),
        pl.BlockSpec((64, 128), lambda i: (0, 0)),
    ]


PARAMS = pltpu.CompilerParams(vmem_limit_bytes=32 * 1024 * 1024)


def sums_shape(groups):
    return jax.ShapeDtypeStruct((groups, 2 * MOST, 128), jnp.float32)


SUMS_SPEC = pl.BlockSpec((1, 2 * MOST, 128), lambda i: (i, 0, 0))


def cost(groups):
    return pl.CostEstimate(flops=groups * 300_000_000, bytes_accessed=groups * 400_000, transcendentals=groups * 81920)


def pack_left(strips, start, groups):
    return pl.pallas_call(
        pack_kernel,
        grid=(groups,),
        in_specs=[strip_spec(0, start)],
        out_specs=pl.BlockSpec((2, PATCH, PACKED), lambda i: (i, 0, 0)),
        out_shape=jax.ShapeDtypeStruct((2 * groups, PATCH, PACKED), jnp.bfloat16),
        compiler_params=PARAMS,
    )(strips)


def south_sums(strips, next_top, table_list):
    tiles = strips.shape[0]
    groups = tiles // GROUP
    below = pl.BlockSpec(
        (1, None, None, PATCH, WIDE),
        lambda i: (jnp.minimum(GROUP * i + GROUP, tiles - 1), 0, 1, 0, 0),
    )
    return pl.pallas_call(
        south_kernel,
        grid=(groups,),
        in_specs=[strip_spec(2), strip_spec(1), below, pl.BlockSpec((1, PATCH, WIDE), lambda i: (0, 0, 0))]
        + table_specs(),
        out_specs=SUMS_SPEC,
        out_shape=sums_shape(groups),
        compiler_params=PARAMS,
        cost_estimate=cost(groups),
    )(strips, strips, strips, next_top, *table_list)


def east_sums(strips, packed, start, table_list):
    groups = packed.shape[0] // 2
    return pl.pallas_call(
        east_kernel,
        grid=(groups,),
        in_specs=[strip_spec(3, start), pl.BlockSpec((2, PATCH, PACKED), lambda i: (i, 0, 0))] + table_specs(),
        out_specs=SUMS_SPEC,
        out_shape=sums_shape(groups),
        compiler_params=PARAMS,
        cost_estimate=cost(groups),
    )(strips, packed, *table_list)


def unpack_sums(sums):
    groups = sums.shape[0]
    sums = sums[:, :, :6].reshape(groups, 2, MOST, 3, 2)
    main = sums[:, :, :4].reshape(groups, 2, 2, 2, 3, 2).transpose(0, 1, 2, 4, 3, 5).reshape(groups * 4, 3, 4)
    tail = sums[:, :, 4].transpose(0, 1, 3, 2).reshape(groups * 4, 3, 1)
    return jnp.concatenate([main, tail, jnp.zeros((groups * 4, 3, 3), jnp.float32)], axis=2)


def passed_along(x, axis, by):
    peers = lax.axis_size(axis)
    pairs = [(i, i + by) for i in range(peers) if 0 <= i + by < peers]
    return lax.ppermute(x, axis, pairs)


def edge_tents(offsets, node_count, blocks, patch_len):
    centres = offsets[..., None] + (
        patch_len * jnp.arange(blocks, dtype=jnp.int32) + patch_len // 2
    ).astype(offsets.dtype)
    node_pos = (
        NODE_GAP * jnp.arange(node_count, dtype=jnp.int32).astype(offsets.dtype) + NODE_GAP / 2
    )
    return jnp.maximum(0.0, 1.0 - jnp.abs(centres[..., None] - node_pos) / NODE_GAP)


def spread(tent_table, weight, vectors):
    return jnp.einsum(
        "...kn,...ck->...cn", tent_table * weight[..., None], vectors, precision=HIGHEST_PREC
    )


def edge_force(tent_table, weight, difference):
    projected = jnp.einsum("...kn,...cn->...ck", tent_table, difference, precision=HIGHEST_PREC)
    return spread(tent_table, weight, projected)


def intra_term(mesh_grid, stiffness, anchor_grid):
    count_y, count_x = (mesh_grid.shape[-2], mesh_grid.shape[-1])
    widths = [(0, 0)] * (mesh_grid.ndim - 2) + [(1, 1), (1, 1)]
    padded = jnp.pad(mesh_grid, widths)
    beside = (
        padded[..., :-2, 1:-1]
        + padded[..., 2:, 1:-1]
        + padded[..., 1:-1, :-2]
        + padded[..., 1:-1, 2:]
    )
    row_ids = jnp.arange(count_y, dtype=jnp.int32)[:, None]
    col_ids = jnp.arange(count_x, dtype=jnp.int32)[None, :]
    degree = (
        (row_ids > 0).astype(mesh_grid.dtype)
        + (row_ids < count_y - 1).astype(mesh_grid.dtype)
        + (col_ids > 0).astype(mesh_grid.dtype)
        + (col_ids < count_x - 1).astype(mesh_grid.dtype)
    )
    return stiffness * (degree * mesh_grid - beside) + anchor_grid * mesh_grid


def placed(east_force, west_force, south_force, north_force):
    result = jnp.pad(east_force[..., None], ((0, 0), (0, 0), (0, 0), (MESH_X - 1, 0)))
    result = result - jnp.pad(west_force[..., None], ((0, 0), (0, 0), (0, 0), (0, MESH_X - 1)))
    result = result + jnp.pad(south_force[..., None, :], ((0, 0), (0, 0), (MESH_Y - 1, 0), (0, 0)))
    return result - jnp.pad(north_force[..., None, :], ((0, 0), (0, 0), (0, MESH_Y - 1), (0, 0)))


def cg_weights(moments):
    def dot(p, q):
        return sum(p[i] * q[j] * moments[i + j] for i in range(len(p)) for j in range(len(q)))

    def apply(p):
        return [0.0] + list(p)

    def add(p, scale, q):
        size = max(len(p), len(q))
        p, q = list(p) + [0.0] * (size - len(p)), list(q) + [0.0] * (size - len(q))
        return [a + scale * b for a, b in zip(p, q)]

    one = jnp.ones_like(moments[0])
    residual, direction, positions = [one], [one], [0.0 * one]
    norm = moments[0]
    for iteration in range(3):
        image = apply(direction)
        alpha = norm / dot(direction, image)
        positions = add(positions, alpha, direction)
        residual = add(residual, -alpha, image)
        if iteration < 2:
            norm_next = dot(residual, residual)
            direction = add(residual, norm_next / norm, direction)
            norm = norm_next
    return positions, residual


def per_device(strips, pair_counts, pair_offsets, tile_stiffness, anchor):
    tile_count, patch_len = strips.shape[0], strips.shape[3]
    blocks = strips.shape[4] // patch_len
    table_list = tables()
    groups = tile_count // GROUP
    half = groups // 2
    east_a = passed_along(pack_left(strips, 0, half), "row", -1)
    east_b = passed_along(pack_left(strips, half, groups - half), "row", -1)
    next_top = passed_along(strips[0:1, 0, 1, :, :WIDE], "col", -1)
    south = unpack_sums(south_sums(strips, next_top, table_list))
    east = jnp.concatenate(
        [east_sums(strips, east_a, 0, table_list), east_sums(strips, east_b, half, table_list)], axis=0
    )
    east = unpack_sums(east)
    block_id = jnp.arange(blocks, dtype=jnp.int32)

    def terms(sums, counts, swap):
        weight, total = sums[:, 0], sums[:, 0] + SMALL_WEIGHT
        deep, along = sums[:, 1] / total, sums[:, 2] / total
        shifts = (along, deep) if swap else (deep, along)
        valid = block_id[None, None, :] < counts[:, None, None]
        return jnp.where(valid, jnp.stack((weight,) + shifts, axis=1), 0.0)

    east_terms = terms(east, pair_counts[:, 0, 0], False)
    south_terms = terms(south, pair_counts[:, 0, 1], True)
    match_terms = jnp.stack([east_terms, south_terms], axis=1)
    east_offset = pair_offsets[:, 0, 0].astype(jnp.float32)
    south_offset = pair_offsets[:, 0, 1].astype(jnp.float32)
    south_pack = jnp.concatenate(
        [south_terms, jnp.broadcast_to(south_offset[:, None, None], (tile_count, 1, blocks))], axis=1
    )
    east_pack = jnp.concatenate(
        [east_terms, jnp.broadcast_to(east_offset[:, None, None], (tile_count, 1, blocks))], axis=1
    )
    west_pack = passed_along(east_pack, "row", 1)
    above_last = passed_along(south_pack[tile_count - 1 : tile_count], "col", 1)
    north_pack = jnp.concatenate([above_last, south_pack[: tile_count - 1]], axis=0)
    east_tent = edge_tents(east_offset, MESH_Y, blocks, patch_len)
    west_tent = edge_tents(west_pack[:, 3, 0], MESH_Y, blocks, patch_len)
    south_tent = edge_tents(south_offset, MESH_X, blocks, patch_len)
    north_tent = edge_tents(north_pack[:, 3, 0], MESH_X, blocks, patch_len)
    rhs = placed(
        spread(east_tent, east_terms[:, 0], east_terms[:, 1:]),
        spread(west_tent, west_pack[:, 0], west_pack[:, 1:3]),
        spread(south_tent, south_terms[:, 0], south_terms[:, 1:]),
        spread(north_tent, north_pack[:, 0], north_pack[:, 1:3]),
    )
    stiffness = tile_stiffness[:, 0][:, None, None, None]
    anchor_grid = anchor[:, 0].reshape(tile_count, 1, MESH_Y, MESH_X)

    def operate(grid):
        left, right = grid[..., :, 0], grid[..., :, MESH_X - 1]
        top, bottom = grid[..., 0, :], grid[..., MESH_Y - 1, :]
        east_left = passed_along(left, "row", -1)
        west_right = passed_along(right, "row", 1)
        south_top = jnp.concatenate([top[1:], passed_along(top[:1], "col", -1)], axis=0)
        north_bottom = jnp.concatenate([passed_along(bottom[-1:], "col", 1), bottom[:-1]], axis=0)
        return intra_term(grid, stiffness, anchor_grid) + placed(
            edge_force(east_tent, east_terms[:, 0], right - east_left),
            edge_force(west_tent, west_pack[:, 0], west_right - left),
            edge_force(south_tent, south_terms[:, 0], bottom - south_top),
            edge_force(north_tent, north_pack[:, 0], north_bottom - top),
        )

    basis = [rhs]
    for _ in range(3):
        basis.append(operate(basis[-1]))
    moments = [jnp.sum(basis[k // 2] * basis[(k + 1) // 2]) for k in range(6)]
    moments = lax.psum(jnp.stack(moments), ("row", "col"))
    to_positions, to_residual = cg_weights([moments[k] for k in range(6)])
    positions = sum(c * v for c, v in zip(to_positions, basis))
    residual = sum(c * v for c, v in zip(to_residual, basis))
    flat = (tile_count, 1, 2, MESH_Y * MESH_X)
    return match_terms[:, None], positions.reshape(flat), residual.reshape(flat)


def solution(mesh):
    return jax.shard_map(
        per_device,
        mesh=mesh,
        in_specs=(
            P("col", "row", None, None, None),
            P("col", "row", None),
            P("col", "row", None),
            P("col", "row"),
            P("col", "row", None),
        ),
        out_specs=(
            P("col", "row", None, None, None),
            P("col", "row", None, None),
            P("col", "row", None, None),
        ),
        check_vma=False,
    )
```

```python
import math

import jax
import jax.numpy as jnp
import numpy as np
from jax import lax
from jax.experimental import pallas as pl
from jax.experimental.pallas import tpu as pltpu
from jax.sharding import PartitionSpec as P

MESH_Y = 28
MESH_X = 32
PATCH = 64
MOST = 5
GROUP = 4
WIDE = 384
PACKED = 2 * MOST * PATCH
SMALL_WEIGHT = 1e-06
NODE_GAP = 16.0
HIGHEST_PREC = lax.Precision.HIGHEST


def tables():
    line = np.arange(PATCH)
    angles = (line[:, None] * line[None, :] % PATCH) * (2.0 * math.pi / PATCH)
    cosine, sine = np.cos(angles), np.sin(angles)
    two = np.eye(2)
    cos2, sin2 = np.kron(two, cosine), np.kron(two, sine)
    depth = np.concatenate([cosine, -sine], axis=0)
    length = np.block([[cos2, -sin2], [sin2, cos2]])
    back_length = np.block([[cos2, sin2], [-sin2, cos2]])
    back_depth = np.concatenate([cosine, -sine], axis=1)
    return [jnp.asarray(t, jnp.bfloat16) for t in (depth, length, back_length, back_depth)]


def pack_two(a, b):
    tail = jnp.concatenate([a[:, 256:320], b[:, 256:320]], axis=1)
    return jnp.concatenate([a[:, :256], b[:, :256], tail], axis=1)


def block_sums(first, second, depth_ref, length_ref, back_length_ref, back_depth_ref):
    count = first.shape[1] // 128
    depth_table = depth_ref[...]

    def by_rows(strip):
        half = jnp.dot(depth_table, strip, preferred_element_type=jnp.float32).astype(jnp.bfloat16)
        return [
            jnp.concatenate([half[:64, 128 * j : 128 * j + 128], half[64:, 128 * j : 128 * j + 128]], axis=1)
            for j in range(count)
        ]

    rows = jnp.concatenate(by_rows(first) + by_rows(second), axis=0)
    spec = jnp.dot(rows, length_ref[...], preferred_element_type=jnp.float32)
    half_rows = 64 * count
    ar, ai = spec[:half_rows, :128], spec[:half_rows, 128:]
    br, bi = spec[half_rows:, :128], spec[half_rows:, 128:]
    inverse = 1.0 / (0.5 * (ar * ar + ai * ai + br * br + bi * bi) + 1.0)
    cross_real = ((ar * br + ai * bi) * inverse).astype(jnp.bfloat16)
    cross_imag = ((ai * br - ar * bi) * inverse).astype(jnp.bfloat16)
    cross = jnp.concatenate([cross_real, cross_imag], axis=1)
    back = jnp.dot(cross, back_length_ref[...], preferred_element_type=jnp.float32).astype(jnp.bfloat16)
    columns = jnp.concatenate(
        [
            jnp.concatenate([back[64 * j : 64 * j + 64, :128], back[64 * j : 64 * j + 64, 128:]], axis=0)
            for j in range(count)
        ],
        axis=1,
    )
    surface = jnp.dot(back_depth_ref[...], columns, preferred_element_type=jnp.float32)
    power = surface * surface
    row_id = lax.broadcasted_iota(jnp.int32, (64, 1), 0)
    depth_offset = ((row_id + 32) % 64 - 32).astype(jnp.float32)
    plain = jnp.sum(power, axis=0, keepdims=True)
    deep = jnp.sum(power * depth_offset, axis=0, keepdims=True)
    plain = jnp.concatenate([plain[:, 128 * j : 128 * j + 128] for j in range(count)], axis=0)
    deep = jnp.concatenate([deep[:, 128 * j : 128 * j + 128] for j in range(count)], axis=0)
    lane = lax.broadcasted_iota(jnp.int32, (count, 128), 1)
    along = plain * ((lane % 64 + 32) % 64 - 32).astype(jnp.float32)
    low = lane < 64
    out = jnp.zeros((count, 128), jnp.float32)
    scale = 1.0 / float(PATCH**4)
    for k, value in enumerate((plain, deep, along)):
        even = jnp.sum(jnp.where(low, value, 0.0), axis=1, keepdims=True) * scale
        odd = jnp.sum(jnp.where(low, 0.0, value), axis=1, keepdims=True) * scale
        out = jnp.where(lane == 2 * k, even, out)
        out = jnp.where(lane == 2 * k + 1, odd, out)
    return out


def south_kernel(first_ref, top_ref, below_ref, next_ref, d_ref, l_ref, bl_ref, bd_ref, out_ref):
    last = pl.program_id(0) == pl.num_programs(0) - 1
    lower = jnp.where(last, next_ref[0], below_ref[0])
    first = jnp.concatenate([pack_two(first_ref[0], first_ref[1]), pack_two(first_ref[2], first_ref[3])], axis=1)
    second = jnp.concatenate([pack_two(top_ref[1], top_ref[2]), pack_two(top_ref[3], lower)], axis=1)
    out_ref[0] = block_sums(first, second, d_ref, l_ref, bl_ref, bd_ref)


def east_kernel(first_ref, second_ref, d_ref, l_ref, bl_ref, bd_ref, out_ref):
    first = jnp.concatenate([pack_two(first_ref[0], first_ref[1]), pack_two(first_ref[2], first_ref[3])], axis=1)
    second = jnp.concatenate([second_ref[0], second_ref[1]], axis=1)
    out_ref[0] = block_sums(first, second, d_ref, l_ref, bl_ref, bd_ref)


def pack_kernel(left_ref, out_ref):
    out_ref[0] = pack_two(left_ref[0], left_ref[1])
    out_ref[1] = pack_two(left_ref[2], left_ref[3])


def strip_spec(side, start=0):
    return pl.BlockSpec((GROUP, None, None, PATCH, WIDE), lambda i: (i + start, 0, side, 0, 0))


def table_specs():
    return [
        pl.BlockSpec((128, 64), lambda i: (0, 0)),
        pl.BlockSpec((256, 256), lambda i: (0, 0)),
        pl.BlockSpec((256, 256), lambda i: (0, 0)),
        pl.BlockSpec((64, 128), lambda i: (0, 0)),
    ]


PARAMS = pltpu.CompilerParams(vmem_limit_bytes=32 * 1024 * 1024)


def sums_shape(groups):
    return jax.ShapeDtypeStruct((groups, 2 * MOST, 128), jnp.float32)


SUMS_SPEC = pl.BlockSpec((1, 2 * MOST, 128), lambda i: (i, 0, 0))


def cost(groups):
    return pl.CostEstimate(flops=groups * 300_000_000, bytes_accessed=groups * 400_000, transcendentals=groups * 81920)


def pack_left(strips, start, groups):
    return pl.pallas_call(
        pack_kernel,
        grid=(groups,),
        in_specs=[strip_spec(0, start)],
        out_specs=pl.BlockSpec((2, PATCH, PACKED), lambda i: (i, 0, 0)),
        out_shape=jax.ShapeDtypeStruct((2 * groups, PATCH, PACKED), jnp.bfloat16),
        compiler_params=PARAMS,
    )(strips)


def south_sums(strips, next_top, table_list):
    tiles = strips.shape[0]
    groups = tiles // GROUP
    below = pl.BlockSpec(
        (1, None, None, PATCH, WIDE),
        lambda i: (jnp.minimum(GROUP * i + GROUP, tiles - 1), 0, 1, 0, 0),
    )
    return pl.pallas_call(
        south_kernel,
        grid=(groups,),
        in_specs=[strip_spec(2), strip_spec(1), below, pl.BlockSpec((1, PATCH, WIDE), lambda i: (0, 0, 0))]
        + table_specs(),
        out_specs=SUMS_SPEC,
        out_shape=sums_shape(groups),
        compiler_params=PARAMS,
        cost_estimate=cost(groups),
    )(strips, strips, strips, next_top, *table_list)


def east_sums(strips, packed, start, table_list):
    groups = packed.shape[0] // 2
    return pl.pallas_call(
        east_kernel,
        grid=(groups,),
        in_specs=[strip_spec(3, start), pl.BlockSpec((2, PATCH, PACKED), lambda i: (i, 0, 0))] + table_specs(),
        out_specs=SUMS_SPEC,
        out_shape=sums_shape(groups),
        compiler_params=PARAMS,
        cost_estimate=cost(groups),
    )(strips, packed, *table_list)


def unpack_sums(sums):
    groups = sums.shape[0]
    sums = sums[:, :, :6].reshape(groups, 2, MOST, 3, 2)
    main = sums[:, :, :4].reshape(groups, 2, 2, 2, 3, 2).transpose(0, 1, 2, 4, 3, 5).reshape(groups * 4, 3, 4)
    tail = sums[:, :, 4].transpose(0, 1, 3, 2).reshape(groups * 4, 3, 1)
    return jnp.concatenate([main, tail, jnp.zeros((groups * 4, 3, 3), jnp.float32)], axis=2)


def passed_along(x, axis, by):
    peers = lax.axis_size(axis)
    pairs = [(i, i + by) for i in range(peers) if 0 <= i + by < peers]
    return lax.ppermute(x, axis, pairs)


def edge_selection():
    chosen = np.zeros((MESH_Y * MESH_X, 128), np.float32)
    for i in range(MESH_Y):
        chosen[MESH_X * i, i] = 1.0
        chosen[MESH_X * i + MESH_X - 1, 32 + i] = 1.0
    for j in range(MESH_X):
        chosen[j, 64 + j] = 1.0
        chosen[MESH_X * (MESH_Y - 1) + j, 96 + j] = 1.0
    return chosen


def cg_weights(moments):
    def dot(p, q):
        return sum(
            a * b * moments[i + j]
            for i, a in enumerate(p)
            for j, b in enumerate(q)
            if a is not None and b is not None
        )

    def add(p, scale, q):
        size = max(len(p), len(q))
        p, q = list(p) + [None] * (size - len(p)), list(q) + [None] * (size - len(q))
        return [a if b is None else scale * b if a is None else a + scale * b for a, b in zip(p, q)]

    one = jnp.ones_like(moments[0])
    residual, direction, positions = [one], [one], [None]
    norm = moments[0]
    for iteration in range(3):
        image = [None] + direction
        alpha = norm / dot(direction, image)
        positions = add(positions, alpha, direction)
        residual = add(residual, -alpha, image)
        if iteration < 2:
            norm_next = dot(residual, residual)
            direction = add(residual, norm_next / norm, direction)
            norm = norm_next
    return positions, residual


def cg_kernel(
    rows, cols, terms_ref, stiff_ref, anchor_ref, pick_ref, place_ref, positions_ref, residual_ref,
    pair_send, pair_recv, edge_send, edge_recv, basis, part, part_row, part_col,
    pair_ssem, pair_rsem, edge_ssem, edge_rsem, row_ssem, row_rsem, col_ssem, col_rsem,
):
    my_row, my_col = lax.axis_index("row"), lax.axis_index("col")
    tiles = terms_ref.shape[0]

    def on_row(by):
        return (lax.rem(my_row + by + rows, rows), my_col)

    def on_col(by):
        return (my_row, lax.rem(my_col + by + cols, cols))

    barrier = pltpu.get_barrier_semaphore()
    for by in range(1, rows):
        pl.semaphore_signal(barrier, inc=1, device_id=on_row(by), device_id_type=pl.DeviceIdType.MESH)
    for by in range(1, cols):
        pl.semaphore_signal(barrier, inc=1, device_id=on_col(by), device_id_type=pl.DeviceIdType.MESH)

    def send(source, target, ssem, rsem, device):
        copy = pltpu.make_async_remote_copy(
            src_ref=source, dst_ref=target, send_sem=ssem, recv_sem=rsem,
            device_id=device, device_id_type=pl.DeviceIdType.MESH,
        )
        copy.start()
        return copy

    lane = lax.broadcasted_iota(jnp.int32, (tiles, 128), 1)
    tile_id = lax.broadcasted_iota(jnp.int32, (tiles, 128), 0)
    node = lane % 32
    group = lane // 32
    own = (group % 2) == 1
    node_count = jnp.where(group < 2, MESH_Y, MESH_X)
    inside = own & (node < node_count)
    linked = own & (node < node_count - 1)

    def term(k):
        return jnp.where(group < 2, terms_ref[:, k : k + 1], terms_ref[:, 24 + k : 25 + k])

    offset = jnp.where(group < 2, terms_ref[:, 48:49], terms_ref[:, 49:50])
    node_pos = NODE_GAP * node.astype(jnp.float32) + NODE_GAP / 2
    zero = jnp.zeros((tiles, 128), jnp.float32)
    self_term, link_term, force_x, force_y = zero, zero, zero, zero
    for k in range(MOST):
        centre = offset + float(PATCH * k + PATCH // 2)
        tent = jnp.maximum(0.0, 1.0 - jnp.abs(centre - node_pos) / NODE_GAP)
        after = jnp.maximum(0.0, 1.0 - jnp.abs(centre - node_pos - NODE_GAP) / NODE_GAP)
        weighted = term(k) * tent
        self_term += weighted * tent
        link_term += weighted * after
        force_x += weighted * term(8 + k)
        force_y += weighted * term(16 + k)
    pair_send[0] = jnp.where(inside, self_term, 0.0)
    pair_send[1] = jnp.where(linked, link_term, 0.0)
    pair_send[2] = jnp.where(inside, force_x, 0.0)
    pair_send[3] = jnp.where(inside, force_y, 0.0)
    pl.semaphore_wait(barrier, rows + cols - 2)
    copies = [
        send(pair_send, pair_recv.at[0], pair_ssem.at[0], pair_rsem.at[0], on_row(1)),
        send(pair_send, pair_recv.at[1], pair_ssem.at[1], pair_rsem.at[1], on_col(1)),
    ]
    for copy in copies:
        copy.wait()

    def partners(west, east, own_part, north, south):
        above = jnp.where(tile_id == 0, north[tiles - 1 : tiles], pltpu.roll(own_part, 1, 0))
        low = pltpu.roll(jnp.where(group == 1, west, above), 96, 1)
        if east is None:
            return jnp.where(own, 0.0, low)
        below = jnp.where(tile_id == tiles - 1, south[0:1], pltpu.roll(own_part, tiles - 1, 0))
        high = pltpu.roll(jnp.where(group == 0, east, below), 32, 1)
        return jnp.where(own, high, low)

    others = [partners(pair_recv[0, c], None, pair_send[c], pair_recv[1, c], None) for c in range(4)]
    self_term = pair_send[0] + others[0]
    link_term = pair_send[1] + others[1]
    self_both = jnp.concatenate([self_term, self_term], axis=0)
    link_both = jnp.concatenate([link_term, link_term], axis=0)
    force = jnp.concatenate([pair_send[2] - others[2], pair_send[3] - others[3]], axis=0)

    def expand(values):
        return jnp.dot(values, place_ref[...], preferred_element_type=jnp.float32, precision=HIGHEST_PREC)

    nodes = MESH_Y * MESH_X
    spot = lax.broadcasted_iota(jnp.int32, (1, nodes), 1)
    column = spot % MESH_X
    keep_left = (column > 0).astype(jnp.float32)
    keep_right = (column < MESH_X - 1).astype(jnp.float32)
    keep_up = (spot >= MESH_X).astype(jnp.float32)
    keep_down = (spot < nodes - MESH_X).astype(jnp.float32)
    degree = keep_left + keep_right + keep_up + keep_down
    stiff = jnp.concatenate([stiff_ref[...], stiff_ref[...]], axis=0)
    anchor = jnp.concatenate([anchor_ref[...], anchor_ref[...]], axis=0)

    basis[0] = expand(force)
    for step in range(3):
        field = basis[step]
        edges = jnp.dot(field, pick_ref[...], preferred_element_type=jnp.float32, precision=HIGHEST_PREC)
        edge_send[step] = edges
        copies = [
            send(edge_send.at[step], edge_recv.at[step, d], edge_ssem.at[step, d], edge_rsem.at[step, d], device)
            for d, device in enumerate((on_row(1), on_row(-1), on_col(1), on_col(-1)))
        ]
        beside = (
            keep_left * pltpu.roll(field, 1, 1)
            + keep_right * pltpu.roll(field, nodes - 1, 1)
            + keep_up * pltpu.roll(field, MESH_X, 1)
            + keep_down * pltpu.roll(field, nodes - MESH_X, 1)
        )
        inner = stiff * (degree * field - beside) + anchor * field
        for copy in copies:
            copy.wait()
        partner = jnp.concatenate(
            [
                partners(*[
                    edge_recv[step, 0, c * tiles : (c + 1) * tiles],
                    edge_recv[step, 1, c * tiles : (c + 1) * tiles],
                    edges[c * tiles : (c + 1) * tiles],
                    edge_recv[step, 2, c * tiles : (c + 1) * tiles],
                    edge_recv[step, 3, c * tiles : (c + 1) * tiles],
                ])
                for c in range(2)
            ],
            axis=0,
        )
        gap = edges - partner
        pull = self_both * gap + link_both * pltpu.roll(gap, 127, 1) + pltpu.roll(link_both * gap, 1, 1)
        basis[step + 1] = inner + expand(pull)

    def total(k):
        product = basis[k // 2] * basis[(k + 1) // 2]
        return jnp.sum(jnp.sum(product, axis=0, keepdims=True), axis=1, keepdims=True)

    spots = lax.broadcasted_iota(jnp.int32, (8, 128), 1)
    sums = jnp.zeros((8, 128), jnp.float32)
    for k in range(6):
        sums = jnp.where(spots == k, total(k), sums)
    part[0] = sums
    copies = [
        send(part.at[0], part_row.at[by - 1], row_ssem.at[by - 1], row_rsem.at[by - 1], on_row(by))
        for by in range(1, rows)
    ]
    for by in range(1, rows):
        copies[by - 1].wait()
        sums = sums + part_row[by - 1]
    part[1] = sums
    copies = [
        send(part.at[1], part_col.at[by - 1], col_ssem.at[by - 1], col_rsem.at[by - 1], on_col(by))
        for by in range(1, cols)
    ]
    for by in range(1, cols):
        copies[by - 1].wait()
        sums = sums + part_col[by - 1]
    to_positions, to_residual = cg_weights([sums[0:1, k : k + 1] for k in range(6)])
    positions_ref[...] = sum(c * basis[i] for i, c in enumerate(to_positions))
    residual_ref[...] = sum(c * basis[i] for i, c in enumerate(to_residual))


def mesh_solve(terms, stiffness, anchor):
    rows, cols = lax.axis_size("row"), lax.axis_size("col")
    tiles, nodes = anchor.shape
    chosen = edge_selection()
    vmem = pl.BlockSpec(memory_space=pltpu.VMEM)
    dma = pltpu.SemaphoreType.DMA
    f32 = jnp.float32
    field = jax.ShapeDtypeStruct((2 * tiles, nodes), f32)

    def kernel(*refs):
        cg_kernel(rows, cols, *refs)

    return pl.pallas_call(
        kernel,
        out_shape=(field, field),
        in_specs=[vmem] * 5,
        out_specs=(vmem, vmem),
        scratch_shapes=[
            pltpu.VMEM((4, tiles, 128), f32),
            pltpu.VMEM((2, 4, tiles, 128), f32),
            pltpu.VMEM((3, 2 * tiles, 128), f32),
            pltpu.VMEM((3, 4, 2 * tiles, 128), f32),
            pltpu.VMEM((4, 2 * tiles, nodes), f32),
            pltpu.VMEM((2, 8, 128), f32),
            pltpu.VMEM((rows - 1, 8, 128), f32),
            pltpu.VMEM((cols - 1, 8, 128), f32),
            dma((2,)),
            dma((2,)),
            dma((3, 4)),
            dma((3, 4)),
            dma((rows - 1,)),
            dma((rows - 1,)),
            dma((cols - 1,)),
            dma((cols - 1,)),
        ],
        compiler_params=pltpu.CompilerParams(
            collective_id=0, has_side_effects=True, vmem_limit_bytes=32 * 1024 * 1024
        ),
    )(terms, stiffness, anchor, jnp.asarray(chosen), jnp.asarray(chosen.T))


def per_device(strips, pair_counts, pair_offsets, tile_stiffness, anchor):
    tile_count, patch_len = strips.shape[0], strips.shape[3]
    blocks = strips.shape[4] // patch_len
    table_list = tables()
    groups = tile_count // GROUP
    half = groups // 2
    east_a = passed_along(pack_left(strips, 0, half), "row", -1)
    east_b = passed_along(pack_left(strips, half, groups - half), "row", -1)
    next_top = passed_along(strips[0:1, 0, 1, :, :WIDE], "col", -1)
    south = unpack_sums(south_sums(strips, next_top, table_list))
    east = jnp.concatenate(
        [east_sums(strips, east_a, 0, table_list), east_sums(strips, east_b, half, table_list)], axis=0
    )
    east = unpack_sums(east)
    block_id = jnp.arange(blocks, dtype=jnp.int32)

    def terms(sums, counts, swap):
        weight, total = sums[:, 0], sums[:, 0] + SMALL_WEIGHT
        deep, along = sums[:, 1] / total, sums[:, 2] / total
        shifts = (along, deep) if swap else (deep, along)
        valid = block_id[None, None, :] < counts[:, None, None]
        return jnp.where(valid, jnp.stack((weight,) + shifts, axis=1), 0.0)

    east_terms = terms(east, pair_counts[:, 0, 0], False)
    south_terms = terms(south, pair_counts[:, 0, 1], True)
    match_terms = jnp.stack([east_terms, south_terms], axis=1)
    offsets = pair_offsets[:, 0].astype(jnp.float32)
    table = jnp.concatenate(
        [match_terms.reshape(tile_count, 6 * blocks), offsets, jnp.zeros((tile_count, 126 - 6 * blocks), jnp.float32)],
        axis=1,
    )
    positions, residual = mesh_solve(table, tile_stiffness, anchor[:, 0])
    nodes = MESH_Y * MESH_X

    def by_tile(field):
        return field.reshape(2, tile_count, nodes).transpose(1, 0, 2)[:, None]

    return match_terms[:, None], by_tile(positions), by_tile(residual)


def solution(mesh):
    return jax.shard_map(
        per_device,
        mesh=mesh,
        in_specs=(
            P("col", "row", None, None, None),
            P("col", "row", None),
            P("col", "row", None),
            P("col", "row"),
            P("col", "row", None),
        ),
        out_specs=(
            P("col", "row", None, None, None),
            P("col", "row", None, None),
            P("col", "row", None, None),
        ),
        check_vma=False,
    )
```

```python
import math

import jax
import jax.numpy as jnp
import numpy as np
from jax import lax
from jax.experimental import pallas as pl
from jax.experimental.pallas import tpu as pltpu
from jax.sharding import PartitionSpec as P

MESH_Y = 28
MESH_X = 32
PATCH = 64
MOST = 5
GROUP = 4
WIDE = 384
PACKED = 2 * MOST * PATCH
SMALL_WEIGHT = 1e-06
NODE_GAP = 16.0


def tables():
    line = np.arange(PATCH)
    angles = (line[:, None] * line[None, :] % PATCH) * (2.0 * math.pi / PATCH)
    cosine, sine = np.cos(angles), np.sin(angles)
    two = np.eye(2)
    cos2, sin2 = np.kron(two, cosine), np.kron(two, sine)
    depth = np.concatenate([cosine, -sine], axis=0)
    length = np.block([[cos2, -sin2], [sin2, cos2]])
    back_length = np.block([[cos2, sin2], [-sin2, cos2]])
    back_depth = np.concatenate([cosine, -sine], axis=1)
    return [jnp.asarray(t, jnp.bfloat16) for t in (depth, length, back_length, back_depth)]


def pack_two(a, b):
    tail = jnp.concatenate([a[:, 256:320], b[:, 256:320]], axis=1)
    return jnp.concatenate([a[:, :256], b[:, :256], tail], axis=1)


def block_sums(first, second, depth_ref, length_ref, back_length_ref, back_depth_ref):
    count = first.shape[1] // 128
    depth_table = depth_ref[...]

    def by_rows(strip):
        half = jnp.dot(depth_table, strip, preferred_element_type=jnp.float32).astype(jnp.bfloat16)
        return [
            jnp.concatenate([half[:64, 128 * j : 128 * j + 128], half[64:, 128 * j : 128 * j + 128]], axis=1)
            for j in range(count)
        ]

    rows = jnp.concatenate(by_rows(first) + by_rows(second), axis=0)
    spec = jnp.dot(rows, length_ref[...], preferred_element_type=jnp.float32)
    half_rows = 64 * count
    ar, ai = spec[:half_rows, :128], spec[:half_rows, 128:]
    br, bi = spec[half_rows:, :128], spec[half_rows:, 128:]
    inverse = 1.0 / (0.5 * (ar * ar + ai * ai + br * br + bi * bi) + 1.0)
    cross_real = ((ar * br + ai * bi) * inverse).astype(jnp.bfloat16)
    cross_imag = ((ai * br - ar * bi) * inverse).astype(jnp.bfloat16)
    cross = jnp.concatenate([cross_real, cross_imag], axis=1)
    back = jnp.dot(cross, back_length_ref[...], preferred_element_type=jnp.float32).astype(jnp.bfloat16)
    columns = jnp.concatenate(
        [
            jnp.concatenate([back[64 * j : 64 * j + 64, :128], back[64 * j : 64 * j + 64, 128:]], axis=0)
            for j in range(count)
        ],
        axis=1,
    )
    surface = jnp.dot(back_depth_ref[...], columns, preferred_element_type=jnp.float32)
    power = surface * surface
    row_id = lax.broadcasted_iota(jnp.int32, (64, 1), 0)
    depth_offset = ((row_id + 32) % 64 - 32).astype(jnp.float32)
    plain = jnp.sum(power, axis=0, keepdims=True)
    deep = jnp.sum(power * depth_offset, axis=0, keepdims=True)
    plain = jnp.concatenate([plain[:, 128 * j : 128 * j + 128] for j in range(count)], axis=0)
    deep = jnp.concatenate([deep[:, 128 * j : 128 * j + 128] for j in range(count)], axis=0)
    lane = lax.broadcasted_iota(jnp.int32, (count, 128), 1)
    along = plain * ((lane % 64 + 32) % 64 - 32).astype(jnp.float32)
    low = lane < 64
    out = jnp.zeros((count, 128), jnp.float32)
    scale = 1.0 / float(PATCH**4)
    for k, value in enumerate((plain, deep, along)):
        even = jnp.sum(jnp.where(low, value, 0.0), axis=1, keepdims=True) * scale
        odd = jnp.sum(jnp.where(low, 0.0, value), axis=1, keepdims=True) * scale
        out = jnp.where(lane == 2 * k, even, out)
        out = jnp.where(lane == 2 * k + 1, odd, out)
    return out


def south_kernel(first_ref, top_ref, below_ref, next_ref, d_ref, l_ref, bl_ref, bd_ref, out_ref):
    last = pl.program_id(0) == pl.num_programs(0) - 1
    lower = jnp.where(last, next_ref[0], below_ref[0])
    first = jnp.concatenate([pack_two(first_ref[0], first_ref[1]), pack_two(first_ref[2], first_ref[3])], axis=1)
    second = jnp.concatenate([pack_two(top_ref[1], top_ref[2]), pack_two(top_ref[3], lower)], axis=1)
    out_ref[0] = block_sums(first, second, d_ref, l_ref, bl_ref, bd_ref)


def east_kernel(first_ref, second_ref, d_ref, l_ref, bl_ref, bd_ref, out_ref):
    first = jnp.concatenate([pack_two(first_ref[0], first_ref[1]), pack_two(first_ref[2], first_ref[3])], axis=1)
    second = jnp.concatenate([second_ref[0], second_ref[1]], axis=1)
    out_ref[0] = block_sums(first, second, d_ref, l_ref, bl_ref, bd_ref)


def pack_kernel(left_ref, out_ref):
    out_ref[0] = pack_two(left_ref[0], left_ref[1])
    out_ref[1] = pack_two(left_ref[2], left_ref[3])


def strip_spec(side, start=0):
    return pl.BlockSpec((GROUP, None, None, PATCH, WIDE), lambda i: (i + start, 0, side, 0, 0))


def table_specs():
    return [
        pl.BlockSpec((128, 64), lambda i: (0, 0)),
        pl.BlockSpec((256, 256), lambda i: (0, 0)),
        pl.BlockSpec((256, 256), lambda i: (0, 0)),
        pl.BlockSpec((64, 128), lambda i: (0, 0)),
    ]


PARAMS = pltpu.CompilerParams(vmem_limit_bytes=50 * 1024 * 1024)


def sums_shape(groups):
    return jax.ShapeDtypeStruct((groups, 2 * MOST, 128), jnp.float32)


SUMS_SPEC = pl.BlockSpec((1, 2 * MOST, 128), lambda i: (i, 0, 0))


def cost(groups):
    return pl.CostEstimate(flops=groups * 300_000_000, bytes_accessed=groups * 400_000, transcendentals=groups * 81920)


def pack_left(strips, start, groups):
    return pl.pallas_call(
        pack_kernel,
        grid=(groups,),
        in_specs=[strip_spec(0, start)],
        out_specs=pl.BlockSpec((2, PATCH, PACKED), lambda i: (i, 0, 0)),
        out_shape=jax.ShapeDtypeStruct((2 * groups, PATCH, PACKED), jnp.bfloat16),
        compiler_params=PARAMS,
    )(strips)


def south_sums(strips, next_top, table_list):
    tiles = strips.shape[0]
    groups = tiles // GROUP
    below = pl.BlockSpec(
        (1, None, None, PATCH, WIDE),
        lambda i: (jnp.minimum(GROUP * i + GROUP, tiles - 1), 0, 1, 0, 0),
    )
    return pl.pallas_call(
        south_kernel,
        grid=(groups,),
        in_specs=[strip_spec(2), strip_spec(1), below, pl.BlockSpec((1, PATCH, WIDE), lambda i: (0, 0, 0))]
        + table_specs(),
        out_specs=SUMS_SPEC,
        out_shape=sums_shape(groups),
        compiler_params=PARAMS,
        cost_estimate=cost(groups),
    )(strips, strips, strips, next_top, *table_list)


def east_sums(strips, packed, start, table_list):
    groups = packed.shape[0] // 2
    return pl.pallas_call(
        east_kernel,
        grid=(groups,),
        in_specs=[strip_spec(3, start), pl.BlockSpec((2, PATCH, PACKED), lambda i: (i, 0, 0))] + table_specs(),
        out_specs=SUMS_SPEC,
        out_shape=sums_shape(groups),
        compiler_params=PARAMS,
        cost_estimate=cost(groups),
    )(strips, packed, *table_list)


def unpack_sums(sums):
    groups = sums.shape[0]
    sums = sums[:, :, :6].reshape(groups, 2, MOST, 3, 2)
    main = sums[:, :, :4].reshape(groups, 2, 2, 2, 3, 2).transpose(0, 1, 2, 4, 3, 5).reshape(groups * 4, 3, 4)
    tail = sums[:, :, 4].transpose(0, 1, 3, 2).reshape(groups * 4, 3, 1)
    return jnp.concatenate([main, tail, jnp.zeros((groups * 4, 3, 3), jnp.float32)], axis=2)


def passed_along(x, axis, by):
    peers = lax.axis_size(axis)
    pairs = [(i, i + by) for i in range(peers) if 0 <= i + by < peers]
    return lax.ppermute(x, axis, pairs)


def edge_selection():
    chosen = np.zeros((MESH_Y * MESH_X, 128), np.float32)
    for i in range(MESH_Y):
        chosen[MESH_X * i, i] = 1.0
        chosen[MESH_X * i + MESH_X - 1, 32 + i] = 1.0
    for j in range(MESH_X):
        chosen[j, 64 + j] = 1.0
        chosen[MESH_X * (MESH_Y - 1) + j, 96 + j] = 1.0
    return chosen


def cg_weights(moments):
    def dot(p, q):
        return sum(
            a * b * moments[i + j]
            for i, a in enumerate(p)
            for j, b in enumerate(q)
            if a is not None and b is not None
        )

    def add(p, scale, q):
        size = max(len(p), len(q))
        p, q = list(p) + [None] * (size - len(p)), list(q) + [None] * (size - len(q))
        return [a if b is None else scale * b if a is None else a + scale * b for a, b in zip(p, q)]

    one = jnp.ones_like(moments[0])
    residual, direction, positions = [one], [one], [None]
    norm = moments[0]
    for iteration in range(3):
        image = [None] + direction
        alpha = norm / dot(direction, image)
        positions = add(positions, alpha, direction)
        residual = add(residual, -alpha, image)
        if iteration < 2:
            norm_next = dot(residual, residual)
            direction = add(residual, norm_next / norm, direction)
            norm = norm_next
    return positions, residual


def moved(values, table_ref):
    size = values.shape[0]
    high = values.astype(jnp.bfloat16)
    rest = values - high.astype(jnp.float32)
    middle = rest.astype(jnp.bfloat16)
    low = (rest - middle.astype(jnp.float32)).astype(jnp.bfloat16)
    parts = jnp.concatenate([high, middle, low], axis=0)
    out = jnp.dot(parts, table_ref[...], preferred_element_type=jnp.float32)
    return out[:size] + (out[size : 2 * size] + out[2 * size :])


def cg_kernel(
    rows, cols, terms_ref, stiff_ref, anchor_ref, pick_ref, place_ref, positions_ref, residual_ref,
    pair_send, pair_recv, edge_send, edge_recv, slab_send, slab_recv, basis, part, part_row, part_col,
    pair_ssem, pair_rsem, edge_ssem, edge_rsem, row_ssem, row_rsem, col_ssem, col_rsem,
):
    my_row, my_col = lax.axis_index("row"), lax.axis_index("col")
    tiles = terms_ref.shape[0]

    def on_row(by):
        return (lax.rem(my_row + by + rows, rows), my_col)

    def on_col(by):
        return (my_row, lax.rem(my_col + by + cols, cols))

    barrier = pltpu.get_barrier_semaphore()
    for by in range(1, rows):
        pl.semaphore_signal(barrier, inc=1, device_id=on_row(by), device_id_type=pl.DeviceIdType.MESH)
    for by in range(1, cols):
        pl.semaphore_signal(barrier, inc=1, device_id=on_col(by), device_id_type=pl.DeviceIdType.MESH)

    def send(source, target, ssem, rsem, device):
        copy = pltpu.make_async_remote_copy(
            src_ref=source, dst_ref=target, send_sem=ssem, recv_sem=rsem,
            device_id=device, device_id_type=pl.DeviceIdType.MESH,
        )
        copy.start()
        return copy

    lane = lax.broadcasted_iota(jnp.int32, (tiles, 128), 1)
    tile_id = lax.broadcasted_iota(jnp.int32, (tiles, 128), 0)
    node = lane % 32
    group = lane // 32
    own = (group % 2) == 1
    node_count = jnp.where(group < 2, MESH_Y, MESH_X)
    inside = own & (node < node_count)
    linked = own & (node < node_count - 1)

    def term(k):
        return jnp.where(group < 2, terms_ref[:, k : k + 1], terms_ref[:, 24 + k : 25 + k])

    offset = jnp.where(group < 2, terms_ref[:, 48:49], terms_ref[:, 49:50])
    node_pos = NODE_GAP * node.astype(jnp.float32) + NODE_GAP / 2
    zero = jnp.zeros((tiles, 128), jnp.float32)
    self_term, link_term, force_x, force_y = zero, zero, zero, zero
    for k in range(MOST):
        centre = offset + float(PATCH * k + PATCH // 2)
        tent = jnp.maximum(0.0, 1.0 - jnp.abs(centre - node_pos) / NODE_GAP)
        after = jnp.maximum(0.0, 1.0 - jnp.abs(centre - node_pos - NODE_GAP) / NODE_GAP)
        weighted = term(k) * tent
        self_term += weighted * tent
        link_term += weighted * after
        force_x += weighted * term(8 + k)
        force_y += weighted * term(16 + k)
    pair_send[0] = jnp.where(inside, self_term, 0.0)
    pair_send[1] = jnp.where(linked, link_term, 0.0)
    pair_send[2] = jnp.where(inside, force_x, 0.0)
    pair_send[3] = jnp.where(inside, force_y, 0.0)
    pl.semaphore_wait(barrier, rows + cols - 2)
    copies = [
        send(pair_send, pair_recv.at[0], pair_ssem.at[0], pair_rsem.at[0], on_row(1)),
        send(pair_send, pair_recv.at[1], pair_ssem.at[1], pair_rsem.at[1], on_col(1)),
    ]
    for copy in copies:
        copy.wait()

    def partners(west, east, own_part, north, south):
        above = jnp.where(tile_id == 0, north[-1:], pltpu.roll(own_part, 1, 0))
        low = pltpu.roll(jnp.where(group == 1, west, above), 96, 1)
        if east is None:
            return jnp.where(own, 0.0, low)
        below = jnp.where(tile_id == tiles - 1, south[0:1], pltpu.roll(own_part, tiles - 1, 0))
        high = pltpu.roll(jnp.where(group == 0, east, below), 32, 1)
        return jnp.where(own, high, low)

    others = [partners(pair_recv[0, c], None, pair_send[c], pair_recv[1, c], None) for c in range(4)]
    self_term = pair_send[0] + others[0]
    link_term = pair_send[1] + others[1]
    self_both = jnp.concatenate([self_term, self_term], axis=0)
    link_both = jnp.concatenate([link_term, link_term], axis=0)
    force = jnp.concatenate([pair_send[2] - others[2], pair_send[3] - others[3]], axis=0)

    def expand(values):
        return moved(values, place_ref)

    nodes = MESH_Y * MESH_X
    spot = lax.broadcasted_iota(jnp.int32, (1, nodes), 1)
    column = spot % MESH_X
    keep_left = (column > 0).astype(jnp.float32)
    keep_right = (column < MESH_X - 1).astype(jnp.float32)
    keep_up = (spot >= MESH_X).astype(jnp.float32)
    keep_down = (spot < nodes - MESH_X).astype(jnp.float32)
    degree = keep_left + keep_right + keep_up + keep_down
    stiff = jnp.concatenate([stiff_ref[...], stiff_ref[...]], axis=0)
    anchor = jnp.concatenate([anchor_ref[...], anchor_ref[...]], axis=0)

    basis[0] = expand(force)
    for step in range(3):
        field = basis[step]
        edges = moved(field, pick_ref)
        edge_send[step] = edges
        for c in range(2):
            slab_send[step, 0, 8 * c : 8 * c + 8] = edges[(c + 1) * tiles - 8 : (c + 1) * tiles]
            slab_send[step, 1, 8 * c : 8 * c + 8] = edges[c * tiles : c * tiles + 8]
        copies = [
            send(edge_send.at[step], edge_recv.at[step, d], edge_ssem.at[step, d], edge_rsem.at[step, d], on_row(by))
            for d, by in enumerate((1, -1))
        ] + [
            send(slab_send.at[step, d], slab_recv.at[step, d], edge_ssem.at[step, 2 + d], edge_rsem.at[step, 2 + d], on_col(by))
            for d, by in enumerate((1, -1))
        ]
        beside = (
            keep_left * pltpu.roll(field, 1, 1)
            + keep_right * pltpu.roll(field, nodes - 1, 1)
            + keep_up * pltpu.roll(field, MESH_X, 1)
            + keep_down * pltpu.roll(field, nodes - MESH_X, 1)
        )
        inner = stiff * (degree * field - beside) + anchor * field
        for copy in copies:
            copy.wait()
        partner = jnp.concatenate(
            [
                partners(*[
                    edge_recv[step, 0, c * tiles : (c + 1) * tiles],
                    edge_recv[step, 1, c * tiles : (c + 1) * tiles],
                    edges[c * tiles : (c + 1) * tiles],
                    slab_recv[step, 0, 8 * c : 8 * c + 8],
                    slab_recv[step, 1, 8 * c : 8 * c + 8],
                ])
                for c in range(2)
            ],
            axis=0,
        )
        gap = edges - partner
        pull = self_both * gap + link_both * pltpu.roll(gap, 127, 1) + pltpu.roll(link_both * gap, 1, 1)
        basis[step + 1] = inner + expand(pull)

    def total(k):
        product = basis[k // 2] * basis[(k + 1) // 2]
        return jnp.sum(jnp.sum(product, axis=0, keepdims=True), axis=1, keepdims=True)

    spots = lax.broadcasted_iota(jnp.int32, (8, 128), 1)
    sums = jnp.zeros((8, 128), jnp.float32)
    for k in range(6):
        sums = jnp.where(spots == k, total(k), sums)
    part[0] = sums
    copies = [
        send(part.at[0], part_row.at[by - 1], row_ssem.at[by - 1], row_rsem.at[by - 1], on_row(by))
        for by in range(1, rows)
    ]
    for by in range(1, rows):
        copies[by - 1].wait()
        sums = sums + part_row[by - 1]
    part[1] = sums
    copies = [
        send(part.at[1], part_col.at[by - 1], col_ssem.at[by - 1], col_rsem.at[by - 1], on_col(by))
        for by in range(1, cols)
    ]
    for by in range(1, cols):
        copies[by - 1].wait()
        sums = sums + part_col[by - 1]
    to_positions, to_residual = cg_weights([sums[0:1, k : k + 1] for k in range(6)])
    positions_ref[...] = sum(c * basis[i] for i, c in enumerate(to_positions))
    residual_ref[...] = sum(c * basis[i] for i, c in enumerate(to_residual))


def mesh_solve(terms, stiffness, anchor):
    rows, cols = lax.axis_size("row"), lax.axis_size("col")
    tiles, nodes = anchor.shape
    chosen = edge_selection()
    vmem = pl.BlockSpec(memory_space=pltpu.VMEM)
    dma = pltpu.SemaphoreType.DMA
    f32 = jnp.float32
    field = jax.ShapeDtypeStruct((2 * tiles, nodes), f32)

    def kernel(*refs):
        cg_kernel(rows, cols, *refs)

    return pl.pallas_call(
        kernel,
        out_shape=(field, field),
        in_specs=[vmem] * 5,
        out_specs=(vmem, vmem),
        scratch_shapes=[
            pltpu.VMEM((4, tiles, 128), f32),
            pltpu.VMEM((2, 4, tiles, 128), f32),
            pltpu.VMEM((3, 2 * tiles, 128), f32),
            pltpu.VMEM((3, 2, 2 * tiles, 128), f32),
            pltpu.VMEM((3, 2, 16, 128), f32),
            pltpu.VMEM((3, 2, 16, 128), f32),
            pltpu.VMEM((4, 2 * tiles, nodes), f32),
            pltpu.VMEM((2, 8, 128), f32),
            pltpu.VMEM((rows - 1, 8, 128), f32),
            pltpu.VMEM((cols - 1, 8, 128), f32),
            dma((2,)),
            dma((2,)),
            dma((3, 4)),
            dma((3, 4)),
            dma((rows - 1,)),
            dma((rows - 1,)),
            dma((cols - 1,)),
            dma((cols - 1,)),
        ],
        compiler_params=pltpu.CompilerParams(
            collective_id=0, has_side_effects=True, vmem_limit_bytes=50 * 1024 * 1024
        ),
    )(terms, stiffness, anchor, jnp.asarray(chosen, jnp.bfloat16), jnp.asarray(chosen.T, jnp.bfloat16))


def per_device(strips, pair_counts, pair_offsets, tile_stiffness, anchor):
    tile_count, patch_len = strips.shape[0], strips.shape[3]
    blocks = strips.shape[4] // patch_len
    table_list = tables()
    groups = tile_count // GROUP
    half = groups - 2 * groups // 5
    east_a = passed_along(pack_left(strips, 0, half), "row", -1)
    east_b = passed_along(pack_left(strips, half, groups - half), "row", -1)
    next_top = passed_along(strips[0:1, 0, 1, :, :WIDE], "col", -1)
    south = unpack_sums(south_sums(strips, next_top, table_list))
    sums_a = east_sums(strips, east_a, 0, table_list)
    east_b, sums_a = lax.optimization_barrier((east_b, sums_a))
    east = jnp.concatenate([sums_a, east_sums(strips, east_b, half, table_list)], axis=0)
    east = unpack_sums(east)
    block_id = jnp.arange(blocks, dtype=jnp.int32)

    def terms(sums, counts, swap):
        weight, total = sums[:, 0], sums[:, 0] + SMALL_WEIGHT
        deep, along = sums[:, 1] / total, sums[:, 2] / total
        shifts = (along, deep) if swap else (deep, along)
        valid = block_id[None, None, :] < counts[:, None, None]
        return jnp.where(valid, jnp.stack((weight,) + shifts, axis=1), 0.0)

    east_terms = terms(east, pair_counts[:, 0, 0], False)
    south_terms = terms(south, pair_counts[:, 0, 1], True)
    match_terms = jnp.stack([east_terms, south_terms], axis=1)
    offsets = pair_offsets[:, 0].astype(jnp.float32)
    table = jnp.concatenate(
        [match_terms.reshape(tile_count, 6 * blocks), offsets, jnp.zeros((tile_count, 126 - 6 * blocks), jnp.float32)],
        axis=1,
    )
    positions, residual = mesh_solve(table, tile_stiffness, anchor[:, 0])
    nodes = MESH_Y * MESH_X

    def by_tile(field):
        return field.reshape(2, tile_count, nodes).transpose(1, 0, 2)[:, None]

    return match_terms[:, None], by_tile(positions), by_tile(residual)


def solution(mesh):
    return jax.shard_map(
        per_device,
        mesh=mesh,
        in_specs=(
            P("col", "row", None, None, None),
            P("col", "row", None),
            P("col", "row", None),
            P("col", "row"),
            P("col", "row", None),
        ),
        out_specs=(
            P("col", "row", None, None, None),
            P("col", "row", None, None),
            P("col", "row", None, None),
        ),
        check_vma=False,
    )
```

```python
import math

import jax
import jax.numpy as jnp
import numpy as np
from jax import lax
from jax.experimental import pallas as pl
from jax.experimental.pallas import tpu as pltpu
from jax.sharding import PartitionSpec as P

MESH_Y = 28
MESH_X = 32
PATCH = 64
MOST = 5
GROUP = 4
WIDE = 384
PACKED = 2 * MOST * PATCH
SMALL_WEIGHT = 1e-06
NODE_GAP = 16.0


def tables():
    line = np.arange(PATCH)
    angles = (line[:, None] * line[None, :] % PATCH) * (2.0 * math.pi / PATCH)
    cosine, sine = np.cos(angles), np.sin(angles)
    two = np.eye(2)
    cos2, sin2 = np.kron(two, cosine), np.kron(two, sine)
    depth = np.concatenate([cosine, -sine], axis=0)
    length = np.block([[cos2, -sin2], [sin2, cos2]])
    back_length = np.block([[cos2, sin2], [-sin2, cos2]])
    back_depth = np.concatenate([cosine, -sine], axis=1)
    return [jnp.asarray(t, jnp.bfloat16) for t in (depth, length, back_length, back_depth)]


def pack_two(a, b):
    tail = jnp.concatenate([a[:, 256:320], b[:, 256:320]], axis=1)
    return jnp.concatenate([a[:, :256], b[:, :256], tail], axis=1)


def block_sums(first, second, depth_ref, length_ref, back_length_ref, back_depth_ref):
    count = first.shape[1] // 128
    depth_table = depth_ref[...]

    def by_rows(strip):
        half = jnp.dot(depth_table, strip, preferred_element_type=jnp.float32).astype(jnp.bfloat16)
        return [
            jnp.concatenate([half[:64, 128 * j : 128 * j + 128], half[64:, 128 * j : 128 * j + 128]], axis=1)
            for j in range(count)
        ]

    rows = jnp.concatenate(by_rows(first) + by_rows(second), axis=0)
    spec = jnp.dot(rows, length_ref[...], preferred_element_type=jnp.float32)
    half_rows = 64 * count
    ar, ai = spec[:half_rows, :128], spec[:half_rows, 128:]
    br, bi = spec[half_rows:, :128], spec[half_rows:, 128:]
    inverse = 1.0 / (0.5 * (ar * ar + ai * ai + br * br + bi * bi) + 1.0)
    cross_real = ((ar * br + ai * bi) * inverse).astype(jnp.bfloat16)
    cross_imag = ((ai * br - ar * bi) * inverse).astype(jnp.bfloat16)
    cross = jnp.concatenate([cross_real, cross_imag], axis=1)
    back = jnp.dot(cross, back_length_ref[...], preferred_element_type=jnp.float32).astype(jnp.bfloat16)
    columns = jnp.concatenate(
        [
            jnp.concatenate([back[64 * j : 64 * j + 64, :128], back[64 * j : 64 * j + 64, 128:]], axis=0)
            for j in range(count)
        ],
        axis=1,
    )
    surface = jnp.dot(back_depth_ref[...], columns, preferred_element_type=jnp.float32)
    power = surface * surface
    row_id = lax.broadcasted_iota(jnp.int32, (64, 1), 0)
    depth_offset = ((row_id + 32) % 64 - 32).astype(jnp.float32)
    plain = jnp.sum(power, axis=0, keepdims=True)
    deep = jnp.sum(power * depth_offset, axis=0, keepdims=True)
    plain = jnp.concatenate([plain[:, 128 * j : 128 * j + 128] for j in range(count)], axis=0)
    deep = jnp.concatenate([deep[:, 128 * j : 128 * j + 128] for j in range(count)], axis=0)
    lane = lax.broadcasted_iota(jnp.int32, (count, 128), 1)
    along = plain * ((lane % 64 + 32) % 64 - 32).astype(jnp.float32)
    low = lane < 64
    out = jnp.zeros((count, 128), jnp.float32)
    scale = 1.0 / float(PATCH**4)
    for k, value in enumerate((plain, deep, along)):
        even = jnp.sum(jnp.where(low, value, 0.0), axis=1, keepdims=True) * scale
        odd = jnp.sum(jnp.where(low, 0.0, value), axis=1, keepdims=True) * scale
        out = jnp.where(lane == 2 * k, even, out)
        out = jnp.where(lane == 2 * k + 1, odd, out)
    return out


def south_kernel(first_ref, top_ref, below_ref, next_ref, d_ref, l_ref, bl_ref, bd_ref, out_ref):
    last = pl.program_id(0) == pl.num_programs(0) - 1
    lower = jnp.where(last, next_ref[0], below_ref[0])
    first = jnp.concatenate([pack_two(first_ref[0], first_ref[1]), pack_two(first_ref[2], first_ref[3])], axis=1)
    second = jnp.concatenate([pack_two(top_ref[1], top_ref[2]), pack_two(top_ref[3], lower)], axis=1)
    out_ref[0] = block_sums(first, second, d_ref, l_ref, bl_ref, bd_ref)


def east_kernel(first_ref, second_ref, d_ref, l_ref, bl_ref, bd_ref, out_ref):
    first = jnp.concatenate([pack_two(first_ref[0], first_ref[1]), pack_two(first_ref[2], first_ref[3])], axis=1)
    second = jnp.concatenate([second_ref[0], second_ref[1]], axis=1)
    out_ref[0] = block_sums(first, second, d_ref, l_ref, bl_ref, bd_ref)


def pack_kernel(left_ref, out_ref):
    out_ref[0] = pack_two(left_ref[0], left_ref[1])
    out_ref[1] = pack_two(left_ref[2], left_ref[3])


def strip_spec(side, start=0):
    return pl.BlockSpec((GROUP, None, None, PATCH, WIDE), lambda i: (i + start, 0, side, 0, 0))


def table_specs():
    return [
        pl.BlockSpec((128, 64), lambda i: (0, 0)),
        pl.BlockSpec((256, 256), lambda i: (0, 0)),
        pl.BlockSpec((256, 256), lambda i: (0, 0)),
        pl.BlockSpec((64, 128), lambda i: (0, 0)),
    ]


PARAMS = pltpu.CompilerParams(vmem_limit_bytes=50 * 1024 * 1024)


def sums_shape(groups):
    return jax.ShapeDtypeStruct((groups, 2 * MOST, 128), jnp.float32)


SUMS_SPEC = pl.BlockSpec((1, 2 * MOST, 128), lambda i: (i, 0, 0))


def cost(groups):
    return pl.CostEstimate(flops=groups * 300_000_000, bytes_accessed=groups * 400_000, transcendentals=groups * 81920)


def pack_left(strips, start, groups):
    return pl.pallas_call(
        pack_kernel,
        grid=(groups,),
        in_specs=[strip_spec(0, start)],
        out_specs=pl.BlockSpec((2, PATCH, PACKED), lambda i: (i, 0, 0)),
        out_shape=jax.ShapeDtypeStruct((2 * groups, PATCH, PACKED), jnp.bfloat16),
        compiler_params=PARAMS,
    )(strips)


def south_sums(strips, next_top, table_list):
    tiles = strips.shape[0]
    groups = tiles // GROUP
    below = pl.BlockSpec(
        (1, None, None, PATCH, WIDE),
        lambda i: (jnp.minimum(GROUP * i + GROUP, tiles - 1), 0, 1, 0, 0),
    )
    return pl.pallas_call(
        south_kernel,
        grid=(groups,),
        in_specs=[strip_spec(2), strip_spec(1), below, pl.BlockSpec((1, PATCH, WIDE), lambda i: (0, 0, 0))]
        + table_specs(),
        out_specs=SUMS_SPEC,
        out_shape=sums_shape(groups),
        compiler_params=PARAMS,
        cost_estimate=cost(groups),
    )(strips, strips, strips, next_top, *table_list)


def east_sums(strips, packed, start, table_list):
    groups = packed.shape[0] // 2
    return pl.pallas_call(
        east_kernel,
        grid=(groups,),
        in_specs=[strip_spec(3, start), pl.BlockSpec((2, PATCH, PACKED), lambda i: (i, 0, 0))] + table_specs(),
        out_specs=SUMS_SPEC,
        out_shape=sums_shape(groups),
        compiler_params=PARAMS,
        cost_estimate=cost(groups),
    )(strips, packed, *table_list)


def unpack_sums(sums):
    groups = sums.shape[0]
    sums = sums[:, :, :6].reshape(groups, 2, MOST, 3, 2)
    main = sums[:, :, :4].reshape(groups, 2, 2, 2, 3, 2).transpose(0, 1, 2, 4, 3, 5).reshape(groups * 4, 3, 4)
    tail = sums[:, :, 4].transpose(0, 1, 3, 2).reshape(groups * 4, 3, 1)
    return jnp.concatenate([main, tail, jnp.zeros((groups * 4, 3, 3), jnp.float32)], axis=2)


def passed_along(x, axis, by):
    peers = lax.axis_size(axis)
    pairs = [(i, i + by) for i in range(peers) if 0 <= i + by < peers]
    return lax.ppermute(x, axis, pairs)


def edge_selection():
    chosen = np.zeros((MESH_Y * MESH_X, 128), np.float32)
    for i in range(MESH_Y):
        chosen[MESH_X * i, i] = 1.0
        chosen[MESH_X * i + MESH_X - 1, 32 + i] = 1.0
    for j in range(MESH_X):
        chosen[j, 64 + j] = 1.0
        chosen[MESH_X * (MESH_Y - 1) + j, 96 + j] = 1.0
    return chosen


def cg_weights(moments):
    def dot(p, q):
        return sum(
            a * b * moments[i + j]
            for i, a in enumerate(p)
            for j, b in enumerate(q)
            if a is not None and b is not None
        )

    def add(p, scale, q):
        size = max(len(p), len(q))
        p, q = list(p) + [None] * (size - len(p)), list(q) + [None] * (size - len(q))
        return [a if b is None else scale * b if a is None else a + scale * b for a, b in zip(p, q)]

    one = jnp.ones_like(moments[0])
    residual, direction, positions = [one], [one], [None]
    norm = moments[0]
    for iteration in range(3):
        image = [None] + direction
        alpha = norm / dot(direction, image)
        positions = add(positions, alpha, direction)
        residual = add(residual, -alpha, image)
        if iteration < 2:
            norm_next = dot(residual, residual)
            direction = add(residual, norm_next / norm, direction)
            norm = norm_next
    return positions, residual


def moved(values, table_ref):
    size = values.shape[0]
    high = values.astype(jnp.bfloat16)
    rest = values - high.astype(jnp.float32)
    middle = rest.astype(jnp.bfloat16)
    low = (rest - middle.astype(jnp.float32)).astype(jnp.bfloat16)
    parts = jnp.concatenate([high, middle, low], axis=0)
    out = jnp.dot(parts, table_ref[...], preferred_element_type=jnp.float32)
    return out[:size] + (out[size : 2 * size] + out[2 * size :])


def cg_kernel(
    rows, cols, terms_ref, stiff_ref, anchor_ref, pick_ref, place_ref, positions_ref, residual_ref,
    pair_send, below_send, pair_recv, below_recv, edge_send, edge_recv, slab_send, slab_recv, basis, part, part_row, part_col,
    pair_ssem, pair_rsem, edge_ssem, edge_rsem, row_ssem, row_rsem, col_ssem, col_rsem,
):
    my_row, my_col = lax.axis_index("row"), lax.axis_index("col")
    tiles = terms_ref.shape[0]

    def on_row(by):
        return (lax.rem(my_row + by + rows, rows), my_col)

    def on_col(by):
        return (my_row, lax.rem(my_col + by + cols, cols))

    barrier = pltpu.get_barrier_semaphore()
    for by in range(1, rows):
        pl.semaphore_signal(barrier, inc=1, device_id=on_row(by), device_id_type=pl.DeviceIdType.MESH)
    for by in range(1, cols):
        pl.semaphore_signal(barrier, inc=1, device_id=on_col(by), device_id_type=pl.DeviceIdType.MESH)

    def send(source, target, ssem, rsem, device):
        copy = pltpu.make_async_remote_copy(
            src_ref=source, dst_ref=target, send_sem=ssem, recv_sem=rsem,
            device_id=device, device_id_type=pl.DeviceIdType.MESH,
        )
        copy.start()
        return copy

    lane = lax.broadcasted_iota(jnp.int32, (tiles, 128), 1)
    tile_id = lax.broadcasted_iota(jnp.int32, (tiles, 128), 0)
    node = lane % 32
    group = lane // 32
    own = (group % 2) == 1
    node_count = jnp.where(group < 2, MESH_Y, MESH_X)
    inside = own & (node < node_count)
    linked = own & (node < node_count - 1)

    def term(k):
        return jnp.where(group < 2, terms_ref[:, k : k + 1], terms_ref[:, 24 + k : 25 + k])

    offset = jnp.where(group < 2, terms_ref[:, 48:49], terms_ref[:, 49:50])
    node_pos = NODE_GAP * node.astype(jnp.float32) + NODE_GAP / 2
    zero = jnp.zeros((tiles, 128), jnp.float32)
    self_term, link_term, force_x, force_y = zero, zero, zero, zero
    for k in range(MOST):
        centre = offset + float(PATCH * k + PATCH // 2)
        tent = jnp.maximum(0.0, 1.0 - jnp.abs(centre - node_pos) / NODE_GAP)
        after = jnp.maximum(0.0, 1.0 - jnp.abs(centre - node_pos - NODE_GAP) / NODE_GAP)
        weighted = term(k) * tent
        self_term += weighted * tent
        link_term += weighted * after
        force_x += weighted * term(8 + k)
        force_y += weighted * term(16 + k)
    quantities = [
        jnp.where(inside, self_term, 0.0),
        jnp.where(linked, link_term, 0.0),
        jnp.where(inside, force_x, 0.0),
        jnp.where(inside, force_y, 0.0),
    ]

    def turned(values, by):
        return pltpu.roll(values, by % 128, 1) if by % 128 else values

    def by_group(choices):
        out = choices[0]
        for g in range(1, 4):
            out = jnp.where(group == g, choices[g], out)
        return out

    pair_send[...] = by_group([turned(q, 32 * c - 32) for c, q in enumerate(quantities)])
    below_send[...] = by_group([turned(q, 32 * c - 96) for c, q in enumerate(quantities)])[tiles - 8 :]
    pl.semaphore_wait(barrier, rows + cols - 2)
    copies = [
        send(pair_send, pair_recv, pair_ssem.at[0], pair_rsem.at[0], on_row(1)),
        send(below_send, below_recv, pair_ssem.at[1], pair_rsem.at[1], on_col(1)),
    ]
    for copy in copies:
        copy.wait()
    others = []
    for c, q in enumerate(quantities):
        first = turned(below_recv[...], 64 - 32 * c)[7:8]
        above = jnp.where(tile_id == 0, first, turned(pltpu.roll(q, 1, 0), -32))
        others.append(by_group([turned(pair_recv[...], -32 * c), zero, above, zero]))
    self_term = quantities[0] + others[0]
    link_term = quantities[1] + others[1]
    self_both = jnp.concatenate([self_term, self_term], axis=0)
    link_both = jnp.concatenate([link_term, link_term], axis=0)
    force = jnp.concatenate([quantities[2] - others[2], quantities[3] - others[3]], axis=0)

    def expand(values):
        return moved(values, place_ref)

    nodes = MESH_Y * MESH_X
    spot = lax.broadcasted_iota(jnp.int32, (1, nodes), 1)
    column = spot % MESH_X
    keep_left = (column > 0).astype(jnp.float32)
    keep_right = (column < MESH_X - 1).astype(jnp.float32)
    keep_up = (spot >= MESH_X).astype(jnp.float32)
    keep_down = (spot < nodes - MESH_X).astype(jnp.float32)
    degree = keep_left + keep_right + keep_up + keep_down
    stiff = jnp.concatenate([stiff_ref[...], stiff_ref[...]], axis=0)
    anchor = jnp.concatenate([anchor_ref[...], anchor_ref[...]], axis=0)

    basis[0] = expand(force)
    for step in range(3):
        field = basis[step]
        edges = moved(field, pick_ref)
        split = [edges[:tiles], edges[tiles:]]
        edge_send[step, 0] = jnp.where(group == 0, turned(split[0], -32), split[1])
        edge_send[step, 1] = jnp.where(group == 0, split[0], turned(split[1], 32))
        for c in range(2):
            slab_send[step, 0, 8 * c : 8 * c + 8] = edges[(c + 1) * tiles - 8 : (c + 1) * tiles]
            slab_send[step, 1, 8 * c : 8 * c + 8] = edges[c * tiles : c * tiles + 8]
        copies = [
            send(edge_send.at[step, d], edge_recv.at[step, d], edge_ssem.at[step, d], edge_rsem.at[step, d], on_row(by))
            for d, by in enumerate((1, -1))
        ] + [
            send(slab_send.at[step, d], slab_recv.at[step, d], edge_ssem.at[step, 2 + d], edge_rsem.at[step, 2 + d], on_col(by))
            for d, by in enumerate((1, -1))
        ]
        beside = (
            keep_left * pltpu.roll(field, 1, 1)
            + keep_right * pltpu.roll(field, nodes - 1, 1)
            + keep_up * pltpu.roll(field, MESH_X, 1)
            + keep_down * pltpu.roll(field, nodes - MESH_X, 1)
        )
        inner = stiff * (degree * field - beside) + anchor * field
        for copy in copies:
            copy.wait()
        partner = []
        for c in range(2):
            north = slab_recv[step, 0, 8 * c + 7 : 8 * c + 8]
            south = slab_recv[step, 1, 8 * c : 8 * c + 1]
            above = jnp.where(tile_id == 0, north, pltpu.roll(split[c], 1, 0))
            below = jnp.where(tile_id == tiles - 1, south, pltpu.roll(split[c], tiles - 1, 0))
            west = turned(edge_recv[step, 0], -32 * c)
            east = turned(edge_recv[step, 1], 32 - 32 * c)
            partner.append(by_group([west, east, turned(above, -32), turned(below, 32)]))
        partner = jnp.concatenate(partner, axis=0)
        gap = edges - partner
        pull = self_both * gap + link_both * pltpu.roll(gap, 127, 1) + pltpu.roll(link_both * gap, 1, 1)
        basis[step + 1] = inner + expand(pull)

    def total(k):
        product = basis[k // 2] * basis[(k + 1) // 2]
        return jnp.sum(jnp.sum(product, axis=0, keepdims=True), axis=1, keepdims=True)

    spots = lax.broadcasted_iota(jnp.int32, (8, 128), 1)
    sums = jnp.zeros((8, 128), jnp.float32)
    for k in range(6):
        sums = jnp.where(spots == k, total(k), sums)
    part[0] = sums
    copies = [
        send(part.at[0], part_row.at[by - 1], row_ssem.at[by - 1], row_rsem.at[by - 1], on_row(by))
        for by in range(1, rows)
    ]
    for by in range(1, rows):
        copies[by - 1].wait()
        sums = sums + part_row[by - 1]
    part[1] = sums
    copies = [
        send(part.at[1], part_col.at[by - 1], col_ssem.at[by - 1], col_rsem.at[by - 1], on_col(by))
        for by in range(1, cols)
    ]
    for by in range(1, cols):
        copies[by - 1].wait()
        sums = sums + part_col[by - 1]
    to_positions, to_residual = cg_weights([sums[0:1, k : k + 1] for k in range(6)])
    positions_ref[...] = sum(c * basis[i] for i, c in enumerate(to_positions))
    residual_ref[...] = sum(c * basis[i] for i, c in enumerate(to_residual))


def mesh_solve(terms, stiffness, anchor):
    rows, cols = lax.axis_size("row"), lax.axis_size("col")
    tiles, nodes = anchor.shape
    chosen = edge_selection()
    vmem = pl.BlockSpec(memory_space=pltpu.VMEM)
    dma = pltpu.SemaphoreType.DMA
    f32 = jnp.float32
    field = jax.ShapeDtypeStruct((2 * tiles, nodes), f32)

    def kernel(*refs):
        cg_kernel(rows, cols, *refs)

    return pl.pallas_call(
        kernel,
        out_shape=(field, field),
        in_specs=[vmem] * 5,
        out_specs=(vmem, vmem),
        scratch_shapes=[
            pltpu.VMEM((tiles, 128), f32),
            pltpu.VMEM((8, 128), f32),
            pltpu.VMEM((tiles, 128), f32),
            pltpu.VMEM((8, 128), f32),
            pltpu.VMEM((3, 2, tiles, 128), f32),
            pltpu.VMEM((3, 2, tiles, 128), f32),
            pltpu.VMEM((3, 2, 16, 128), f32),
            pltpu.VMEM((3, 2, 16, 128), f32),
            pltpu.VMEM((4, 2 * tiles, nodes), f32),
            pltpu.VMEM((2, 8, 128), f32),
            pltpu.VMEM((rows - 1, 8, 128), f32),
            pltpu.VMEM((cols - 1, 8, 128), f32),
            dma((2,)),
            dma((2,)),
            dma((3, 4)),
            dma((3, 4)),
            dma((rows - 1,)),
            dma((rows - 1,)),
            dma((cols - 1,)),
            dma((cols - 1,)),
        ],
        compiler_params=pltpu.CompilerParams(
            collective_id=0, has_side_effects=True, vmem_limit_bytes=50 * 1024 * 1024
        ),
    )(terms, stiffness, anchor, jnp.asarray(chosen, jnp.bfloat16), jnp.asarray(chosen.T, jnp.bfloat16))


def per_device(strips, pair_counts, pair_offsets, tile_stiffness, anchor):
    tile_count, patch_len = strips.shape[0], strips.shape[3]
    blocks = strips.shape[4] // patch_len
    table_list = tables()
    groups = tile_count // GROUP
    half = groups - 2 * groups // 5
    east_a = passed_along(pack_left(strips, 0, half), "row", -1)
    east_b = passed_along(pack_left(strips, half, groups - half), "row", -1)
    next_top = passed_along(strips[0:1, 0, 1, :, :WIDE], "col", -1)
    south = south_sums(strips, next_top, table_list)
    sums_a = east_sums(strips, east_a, 0, table_list)
    east_b, sums_a = lax.optimization_barrier((east_b, sums_a))
    sums_b = east_sums(strips, east_b, half, table_list)
    sums = unpack_sums(jnp.concatenate([sums_a, sums_b, south], axis=0))
    east, south = sums[:tile_count], sums[tile_count:]
    block_id = jnp.arange(blocks, dtype=jnp.int32)

    def terms(sums, counts, swap):
        weight, total = sums[:, 0], sums[:, 0] + SMALL_WEIGHT
        deep, along = sums[:, 1] / total, sums[:, 2] / total
        shifts = (along, deep) if swap else (deep, along)
        valid = block_id[None, None, :] < counts[:, None, None]
        return jnp.where(valid, jnp.stack((weight,) + shifts, axis=1), 0.0)

    east_terms = terms(east, pair_counts[:, 0, 0], False)
    south_terms = terms(south, pair_counts[:, 0, 1], True)
    match_terms = jnp.stack([east_terms, south_terms], axis=1)
    offsets = pair_offsets[:, 0].astype(jnp.float32)
    table = jnp.concatenate(
        [match_terms.reshape(tile_count, 6 * blocks), offsets, jnp.zeros((tile_count, 126 - 6 * blocks), jnp.float32)],
        axis=1,
    )
    positions, residual = mesh_solve(table, tile_stiffness, anchor[:, 0])
    nodes = MESH_Y * MESH_X

    def by_tile(field):
        return field.reshape(2, tile_count, nodes).transpose(1, 0, 2)[:, None]

    return match_terms[:, None], by_tile(positions), by_tile(residual)


def solution(mesh):
    return jax.shard_map(
        per_device,
        mesh=mesh,
        in_specs=(
            P("col", "row", None, None, None),
            P("col", "row", None),
            P("col", "row", None),
            P("col", "row"),
            P("col", "row", None),
        ),
        out_specs=(
            P("col", "row", None, None, None),
            P("col", "row", None, None),
            P("col", "row", None, None),
        ),
        check_vma=False,
    )
```

```python
import math

import jax
import jax.numpy as jnp
import numpy as np
from jax import lax
from jax.experimental import pallas as pl
from jax.experimental.pallas import tpu as pltpu
from jax.sharding import PartitionSpec as P

MESH_Y = 28
MESH_X = 32
PATCH = 64
MOST = 5
GROUP = 4
WIDE = 384
PACKED = 2 * MOST * PATCH
SMALL_WEIGHT = 1e-06
NODE_GAP = 16.0


def tables():
    line = np.arange(PATCH)
    angles = (line[:, None] * line[None, :] % PATCH) * (2.0 * math.pi / PATCH)
    cosine, sine = np.cos(angles), np.sin(angles)
    two = np.eye(2)
    cos2, sin2 = np.kron(two, cosine), np.kron(two, sine)
    depth = np.concatenate([cosine, -sine], axis=0)
    length = np.block([[cos2, -sin2], [sin2, cos2]])
    back_length = np.block([[cos2, sin2], [-sin2, cos2]])
    back_depth = np.concatenate([cosine, -sine], axis=1)
    return [jnp.asarray(t, jnp.bfloat16) for t in (depth, length, back_length, back_depth)]


def pack_two(a, b):
    tail = jnp.concatenate([a[:, 256:320], b[:, 256:320]], axis=1)
    return jnp.concatenate([a[:, :256], b[:, :256], tail], axis=1)


def block_sums(first, second, depth_ref, length_ref, back_length_ref, back_depth_ref):
    count = first.shape[1] // 128
    depth_table = depth_ref[...]

    def by_rows(strip):
        half = jnp.dot(depth_table, strip, preferred_element_type=jnp.float32).astype(jnp.bfloat16)
        return [
            jnp.concatenate([half[:64, 128 * j : 128 * j + 128], half[64:, 128 * j : 128 * j + 128]], axis=1)
            for j in range(count)
        ]

    rows = jnp.concatenate(by_rows(first) + by_rows(second), axis=0)
    spec = jnp.dot(rows, length_ref[...], preferred_element_type=jnp.float32)
    half_rows = 64 * count
    ar, ai = spec[:half_rows, :128], spec[:half_rows, 128:]
    br, bi = spec[half_rows:, :128], spec[half_rows:, 128:]
    inverse = 1.0 / (0.5 * (ar * ar + ai * ai + br * br + bi * bi) + 1.0)
    cross_real = ((ar * br + ai * bi) * inverse).astype(jnp.bfloat16)
    cross_imag = ((ai * br - ar * bi) * inverse).astype(jnp.bfloat16)
    cross = jnp.concatenate([cross_real, cross_imag], axis=1)
    back = jnp.dot(cross, back_length_ref[...], preferred_element_type=jnp.float32).astype(jnp.bfloat16)
    columns = jnp.concatenate(
        [
            jnp.concatenate([back[64 * j : 64 * j + 64, :128], back[64 * j : 64 * j + 64, 128:]], axis=0)
            for j in range(count)
        ],
        axis=1,
    )
    surface = jnp.dot(back_depth_ref[...], columns, preferred_element_type=jnp.float32)
    power = surface * surface
    row_id = lax.broadcasted_iota(jnp.int32, (64, 1), 0)
    depth_offset = ((row_id + 32) % 64 - 32).astype(jnp.float32)
    plain = jnp.sum(power, axis=0, keepdims=True)
    deep = jnp.sum(power * depth_offset, axis=0, keepdims=True)
    plain = jnp.concatenate([plain[:, 128 * j : 128 * j + 128] for j in range(count)], axis=0)
    deep = jnp.concatenate([deep[:, 128 * j : 128 * j + 128] for j in range(count)], axis=0)
    lane = lax.broadcasted_iota(jnp.int32, (count, 128), 1)
    along = plain * ((lane % 64 + 32) % 64 - 32).astype(jnp.float32)
    low = lane < 64
    out = jnp.zeros((count, 128), jnp.float32)
    scale = 1.0 / float(PATCH**4)
    for k, value in enumerate((plain, deep, along)):
        even = jnp.sum(jnp.where(low, value, 0.0), axis=1, keepdims=True) * scale
        odd = jnp.sum(jnp.where(low, 0.0, value), axis=1, keepdims=True) * scale
        out = jnp.where(lane == 2 * k, even, out)
        out = jnp.where(lane == 2 * k + 1, odd, out)
    return out


def south_kernel(first_ref, top_ref, below_ref, next_ref, d_ref, l_ref, bl_ref, bd_ref, out_ref):
    last = pl.program_id(0) == pl.num_programs(0) - 1
    lower = jnp.where(last, next_ref[0], below_ref[0])
    first = jnp.concatenate([pack_two(first_ref[0], first_ref[1]), pack_two(first_ref[2], first_ref[3])], axis=1)
    second = jnp.concatenate([pack_two(top_ref[1], top_ref[2]), pack_two(top_ref[3], lower)], axis=1)
    out_ref[0] = block_sums(first, second, d_ref, l_ref, bl_ref, bd_ref)


def east_kernel(first_ref, second_ref, d_ref, l_ref, bl_ref, bd_ref, out_ref):
    first = jnp.concatenate([pack_two(first_ref[0], first_ref[1]), pack_two(first_ref[2], first_ref[3])], axis=1)
    second = jnp.concatenate([second_ref[0], second_ref[1]], axis=1)
    out_ref[0] = block_sums(first, second, d_ref, l_ref, bl_ref, bd_ref)


def pack_kernel(left_ref, out_ref):
    for pair in range(GROUP):
        out_ref[pair] = pack_two(left_ref[2 * pair], left_ref[2 * pair + 1])


def strip_spec(side, start=0):
    return pl.BlockSpec((GROUP, None, None, PATCH, WIDE), lambda i: (i + start, 0, side, 0, 0))


def table_specs():
    return [
        pl.BlockSpec((128, 64), lambda i: (0, 0)),
        pl.BlockSpec((256, 256), lambda i: (0, 0)),
        pl.BlockSpec((256, 256), lambda i: (0, 0)),
        pl.BlockSpec((64, 128), lambda i: (0, 0)),
    ]


PARAMS = pltpu.CompilerParams(vmem_limit_bytes=50 * 1024 * 1024)


def sums_shape(groups):
    return jax.ShapeDtypeStruct((groups, 2 * MOST, 128), jnp.float32)


SUMS_SPEC = pl.BlockSpec((1, 2 * MOST, 128), lambda i: (i, 0, 0))


def cost(groups):
    return pl.CostEstimate(flops=groups * 300_000_000, bytes_accessed=groups * 400_000, transcendentals=groups * 81920)


def pack_left(strips, start, groups):
    return pl.pallas_call(
        pack_kernel,
        grid=(groups // 2,),
        in_specs=[pl.BlockSpec((2 * GROUP, None, None, PATCH, WIDE), lambda i: (i + start // 2, 0, 0, 0, 0))],
        out_specs=pl.BlockSpec((GROUP, PATCH, PACKED), lambda i: (i, 0, 0)),
        out_shape=jax.ShapeDtypeStruct((2 * groups, PATCH, PACKED), jnp.bfloat16),
        compiler_params=PARAMS,
    )(strips)


def south_sums(strips, next_top, table_list):
    tiles = strips.shape[0]
    groups = tiles // GROUP
    below = pl.BlockSpec(
        (1, None, None, PATCH, WIDE),
        lambda i: (jnp.minimum(GROUP * i + GROUP, tiles - 1), 0, 1, 0, 0),
    )
    return pl.pallas_call(
        south_kernel,
        grid=(groups,),
        in_specs=[strip_spec(2), strip_spec(1), below, pl.BlockSpec((1, PATCH, WIDE), lambda i: (0, 0, 0))]
        + table_specs(),
        out_specs=SUMS_SPEC,
        out_shape=sums_shape(groups),
        compiler_params=PARAMS,
        cost_estimate=cost(groups),
    )(strips, strips, strips, next_top, *table_list)


def east_sums(strips, packed, start, table_list):
    groups = packed.shape[0] // 2
    return pl.pallas_call(
        east_kernel,
        grid=(groups,),
        in_specs=[strip_spec(3, start), pl.BlockSpec((2, PATCH, PACKED), lambda i: (i, 0, 0))] + table_specs(),
        out_specs=SUMS_SPEC,
        out_shape=sums_shape(groups),
        compiler_params=PARAMS,
        cost_estimate=cost(groups),
    )(strips, packed, *table_list)


def unpack_sums(sums):
    groups = sums.shape[0]
    sums = sums[:, :, :6].reshape(groups, 2, MOST, 3, 2)
    main = sums[:, :, :4].reshape(groups, 2, 2, 2, 3, 2).transpose(0, 1, 2, 4, 3, 5).reshape(groups * 4, 3, 4)
    tail = sums[:, :, 4].transpose(0, 1, 3, 2).reshape(groups * 4, 3, 1)
    return jnp.concatenate([main, tail, jnp.zeros((groups * 4, 3, 3), jnp.float32)], axis=2)


def passed_along(x, axis, by):
    peers = lax.axis_size(axis)
    pairs = [(i, i + by) for i in range(peers) if 0 <= i + by < peers]
    return lax.ppermute(x, axis, pairs)


def edge_selection():
    chosen = np.zeros((MESH_Y * MESH_X, 128), np.float32)
    for i in range(MESH_Y):
        chosen[MESH_X * i, i] = 1.0
        chosen[MESH_X * i + MESH_X - 1, 32 + i] = 1.0
    for j in range(MESH_X):
        chosen[j, 64 + j] = 1.0
        chosen[MESH_X * (MESH_Y - 1) + j, 96 + j] = 1.0
    return chosen


def cg_weights(moments):
    def dot(p, q):
        return sum(
            a * b * moments[i + j]
            for i, a in enumerate(p)
            for j, b in enumerate(q)
            if a is not None and b is not None
        )

    def add(p, scale, q):
        size = max(len(p), len(q))
        p, q = list(p) + [None] * (size - len(p)), list(q) + [None] * (size - len(q))
        return [a if b is None else scale * b if a is None else a + scale * b for a, b in zip(p, q)]

    one = jnp.ones_like(moments[0])
    residual, direction, positions = [one], [one], [None]
    norm = moments[0]
    for iteration in range(3):
        image = [None] + direction
        alpha = norm / dot(direction, image)
        positions = add(positions, alpha, direction)
        residual = add(residual, -alpha, image)
        if iteration < 2:
            norm_next = dot(residual, residual)
            direction = add(residual, norm_next / norm, direction)
            norm = norm_next
    return positions, residual


def moved(values, table_ref):
    size = values.shape[0]
    high = values.astype(jnp.bfloat16)
    rest = values - high.astype(jnp.float32)
    middle = rest.astype(jnp.bfloat16)
    low = (rest - middle.astype(jnp.float32)).astype(jnp.bfloat16)
    parts = jnp.concatenate([high, middle, low], axis=0)
    out = jnp.dot(parts, table_ref[...], preferred_element_type=jnp.float32)
    return out[:size] + (out[size : 2 * size] + out[2 * size :])


def cg_kernel(
    rows, cols, terms_ref, stiff_ref, anchor_ref, pick_ref, place_ref, positions_ref, residual_ref,
    pair_send, below_send, pair_recv, below_recv, edge_send, edge_recv, slab_send, slab_recv, basis, part, part_row, part_col,
    pair_ssem, pair_rsem, edge_ssem, edge_rsem, row_ssem, row_rsem, col_ssem, col_rsem,
):
    my_row, my_col = lax.axis_index("row"), lax.axis_index("col")
    tiles = terms_ref.shape[0]

    def on_row(by):
        return (lax.rem(my_row + by + rows, rows), my_col)

    def on_col(by):
        return (my_row, lax.rem(my_col + by + cols, cols))

    barrier = pltpu.get_barrier_semaphore()
    for by in range(1, rows):
        pl.semaphore_signal(barrier, inc=1, device_id=on_row(by), device_id_type=pl.DeviceIdType.MESH)
    for by in range(1, cols):
        pl.semaphore_signal(barrier, inc=1, device_id=on_col(by), device_id_type=pl.DeviceIdType.MESH)

    def send(source, target, ssem, rsem, device):
        copy = pltpu.make_async_remote_copy(
            src_ref=source, dst_ref=target, send_sem=ssem, recv_sem=rsem,
            device_id=device, device_id_type=pl.DeviceIdType.MESH,
        )
        copy.start()
        return copy

    lane = lax.broadcasted_iota(jnp.int32, (tiles, 128), 1)
    tile_id = lax.broadcasted_iota(jnp.int32, (tiles, 128), 0)
    node = lane % 32
    group = lane // 32
    own = (group % 2) == 1
    node_count = jnp.where(group < 2, MESH_Y, MESH_X)
    inside = own & (node < node_count)
    linked = own & (node < node_count - 1)

    def term(k):
        return jnp.where(group < 2, terms_ref[:, k : k + 1], terms_ref[:, 24 + k : 25 + k])

    offset = jnp.where(group < 2, terms_ref[:, 48:49], terms_ref[:, 49:50])
    node_pos = NODE_GAP * node.astype(jnp.float32) + NODE_GAP / 2
    zero = jnp.zeros((tiles, 128), jnp.float32)
    self_term, link_term, force_x, force_y = zero, zero, zero, zero
    for k in range(MOST):
        centre = offset + float(PATCH * k + PATCH // 2)
        tent = jnp.maximum(0.0, 1.0 - jnp.abs(centre - node_pos) / NODE_GAP)
        after = jnp.maximum(0.0, 1.0 - jnp.abs(centre - node_pos - NODE_GAP) / NODE_GAP)
        weighted = term(k) * tent
        self_term += weighted * tent
        link_term += weighted * after
        force_x += weighted * term(8 + k)
        force_y += weighted * term(16 + k)
    quantities = [
        jnp.where(inside, self_term, 0.0),
        jnp.where(linked, link_term, 0.0),
        jnp.where(inside, force_x, 0.0),
        jnp.where(inside, force_y, 0.0),
    ]

    def turned(values, by):
        return pltpu.roll(values, by % 128, 1) if by % 128 else values

    def by_group(choices):
        out = choices[0]
        for g in range(1, 4):
            out = jnp.where(group == g, choices[g], out)
        return out

    pair_send[...] = by_group([turned(q, 32 * c - 32) for c, q in enumerate(quantities)])
    below_send[...] = by_group([turned(q, 32 * c - 96) for c, q in enumerate(quantities)])[tiles - 8 :]
    pl.semaphore_wait(barrier, rows + cols - 2)
    copies = [
        send(pair_send, pair_recv, pair_ssem.at[0], pair_rsem.at[0], on_row(1)),
        send(below_send, below_recv, pair_ssem.at[1], pair_rsem.at[1], on_col(1)),
    ]
    for copy in copies:
        copy.wait()
    others = []
    for c, q in enumerate(quantities):
        first = turned(below_recv[...], 64 - 32 * c)[7:8]
        above = jnp.where(tile_id == 0, first, turned(pltpu.roll(q, 1, 0), -32))
        others.append(by_group([turned(pair_recv[...], -32 * c), zero, above, zero]))
    self_term = quantities[0] + others[0]
    link_term = quantities[1] + others[1]
    self_both = jnp.concatenate([self_term, self_term], axis=0)
    link_both = jnp.concatenate([link_term, link_term], axis=0)
    force = jnp.concatenate([quantities[2] - others[2], quantities[3] - others[3]], axis=0)

    def expand(values):
        return moved(values, place_ref)

    nodes = MESH_Y * MESH_X
    spot = lax.broadcasted_iota(jnp.int32, (1, nodes), 1)
    column = spot % MESH_X
    keep_left = (column > 0).astype(jnp.float32)
    keep_right = (column < MESH_X - 1).astype(jnp.float32)
    keep_up = (spot >= MESH_X).astype(jnp.float32)
    keep_down = (spot < nodes - MESH_X).astype(jnp.float32)
    degree = keep_left + keep_right + keep_up + keep_down
    stiff = jnp.concatenate([stiff_ref[...], stiff_ref[...]], axis=0)
    anchor = jnp.concatenate([anchor_ref[...], anchor_ref[...]], axis=0)

    basis[0] = expand(force)
    for step in range(3):
        field = basis[step]
        edges = moved(field, pick_ref)
        split = [edges[:tiles], edges[tiles:]]
        edge_send[step, 0] = jnp.where(group == 0, turned(split[0], -32), split[1])
        edge_send[step, 1] = jnp.where(group == 0, split[0], turned(split[1], 32))
        for c in range(2):
            slab_send[step, 0, 8 * c : 8 * c + 8] = edges[(c + 1) * tiles - 8 : (c + 1) * tiles]
            slab_send[step, 1, 8 * c : 8 * c + 8] = edges[c * tiles : c * tiles + 8]
        copies = [
            send(edge_send.at[step, d], edge_recv.at[step, d], edge_ssem.at[step, d], edge_rsem.at[step, d], on_row(by))
            for d, by in enumerate((1, -1))
        ] + [
            send(slab_send.at[step, d], slab_recv.at[step, d], edge_ssem.at[step, 2 + d], edge_rsem.at[step, 2 + d], on_col(by))
            for d, by in enumerate((1, -1))
        ]
        beside = (
            keep_left * pltpu.roll(field, 1, 1)
            + keep_right * pltpu.roll(field, nodes - 1, 1)
            + keep_up * pltpu.roll(field, MESH_X, 1)
            + keep_down * pltpu.roll(field, nodes - MESH_X, 1)
        )
        inner = stiff * (degree * field - beside) + anchor * field
        for copy in copies:
            copy.wait()
        partner = []
        for c in range(2):
            north = slab_recv[step, 0, 8 * c + 7 : 8 * c + 8]
            south = slab_recv[step, 1, 8 * c : 8 * c + 1]
            above = jnp.where(tile_id == 0, north, pltpu.roll(split[c], 1, 0))
            below = jnp.where(tile_id == tiles - 1, south, pltpu.roll(split[c], tiles - 1, 0))
            west = turned(edge_recv[step, 0], -32 * c)
            east = turned(edge_recv[step, 1], 32 - 32 * c)
            partner.append(by_group([west, east, turned(above, -32), turned(below, 32)]))
        partner = jnp.concatenate(partner, axis=0)
        gap = edges - partner
        pull = self_both * gap + link_both * pltpu.roll(gap, 127, 1) + pltpu.roll(link_both * gap, 1, 1)
        basis[step + 1] = inner + expand(pull)

    def total(k):
        product = basis[k // 2] * basis[(k + 1) // 2]
        return jnp.sum(jnp.sum(product, axis=0, keepdims=True), axis=1, keepdims=True)

    spots = lax.broadcasted_iota(jnp.int32, (8, 128), 1)
    sums = jnp.zeros((8, 128), jnp.float32)
    for k in range(6):
        sums = jnp.where(spots == k, total(k), sums)
    part[0] = sums
    copies = [
        send(part.at[0], part_row.at[by - 1], row_ssem.at[by - 1], row_rsem.at[by - 1], on_row(by))
        for by in range(1, rows)
    ]
    for by in range(1, rows):
        copies[by - 1].wait()
        sums = sums + part_row[by - 1]
    part[1] = sums
    copies = [
        send(part.at[1], part_col.at[by - 1], col_ssem.at[by - 1], col_rsem.at[by - 1], on_col(by))
        for by in range(1, cols)
    ]
    for by in range(1, cols):
        copies[by - 1].wait()
        sums = sums + part_col[by - 1]
    to_positions, to_residual = cg_weights([sums[0:1, k : k + 1] for k in range(6)])
    positions_ref[...] = sum(c * basis[i] for i, c in enumerate(to_positions))
    residual_ref[...] = sum(c * basis[i] for i, c in enumerate(to_residual))


def mesh_solve(terms, stiffness, anchor):
    rows, cols = lax.axis_size("row"), lax.axis_size("col")
    tiles, nodes = anchor.shape
    chosen = edge_selection()
    vmem = pl.BlockSpec(memory_space=pltpu.VMEM)
    dma = pltpu.SemaphoreType.DMA
    f32 = jnp.float32
    field = jax.ShapeDtypeStruct((2 * tiles, nodes), f32)

    def kernel(*refs):
        cg_kernel(rows, cols, *refs)

    return pl.pallas_call(
        kernel,
        out_shape=(field, field),
        in_specs=[vmem] * 5,
        out_specs=(vmem, vmem),
        scratch_shapes=[
            pltpu.VMEM((tiles, 128), f32),
            pltpu.VMEM((8, 128), f32),
            pltpu.VMEM((tiles, 128), f32),
            pltpu.VMEM((8, 128), f32),
            pltpu.VMEM((3, 2, tiles, 128), f32),
            pltpu.VMEM((3, 2, tiles, 128), f32),
            pltpu.VMEM((3, 2, 16, 128), f32),
            pltpu.VMEM((3, 2, 16, 128), f32),
            pltpu.VMEM((4, 2 * tiles, nodes), f32),
            pltpu.VMEM((2, 8, 128), f32),
            pltpu.VMEM((rows - 1, 8, 128), f32),
            pltpu.VMEM((cols - 1, 8, 128), f32),
            dma((2,)),
            dma((2,)),
            dma((3, 4)),
            dma((3, 4)),
            dma((rows - 1,)),
            dma((rows - 1,)),
            dma((cols - 1,)),
            dma((cols - 1,)),
        ],
        compiler_params=pltpu.CompilerParams(
            collective_id=0, has_side_effects=True, vmem_limit_bytes=50 * 1024 * 1024
        ),
    )(terms, stiffness, anchor, jnp.asarray(chosen, jnp.bfloat16), jnp.asarray(chosen.T, jnp.bfloat16))


def per_device(strips, pair_counts, pair_offsets, tile_stiffness, anchor):
    tile_count, patch_len = strips.shape[0], strips.shape[3]
    blocks = strips.shape[4] // patch_len
    table_list = tables()
    groups = tile_count // GROUP
    half = groups - 2 * groups // 5
    east_a = passed_along(pack_left(strips, 0, half), "row", -1)
    east_b = passed_along(pack_left(strips, half, groups - half), "row", -1)
    next_top = passed_along(strips[0:1, 0, 1, :, :WIDE], "col", -1)
    south = south_sums(strips, next_top, table_list)
    sums_a = east_sums(strips, east_a, 0, table_list)
    east_b, sums_a = lax.optimization_barrier((east_b, sums_a))
    sums_b = east_sums(strips, east_b, half, table_list)
    sums = unpack_sums(jnp.concatenate([sums_a, sums_b, south], axis=0))
    east, south = sums[:tile_count], sums[tile_count:]
    block_id = jnp.arange(blocks, dtype=jnp.int32)

    def terms(sums, counts, swap):
        weight, total = sums[:, 0], sums[:, 0] + SMALL_WEIGHT
        deep, along = sums[:, 1] / total, sums[:, 2] / total
        shifts = (along, deep) if swap else (deep, along)
        valid = block_id[None, None, :] < counts[:, None, None]
        return jnp.where(valid, jnp.stack((weight,) + shifts, axis=1), 0.0)

    east_terms = terms(east, pair_counts[:, 0, 0], False)
    south_terms = terms(south, pair_counts[:, 0, 1], True)
    match_terms = jnp.stack([east_terms, south_terms], axis=1)
    offsets = pair_offsets[:, 0].astype(jnp.float32)
    table = jnp.concatenate(
        [match_terms.reshape(tile_count, 6 * blocks), offsets],
        axis=1,
    )
    positions, residual = mesh_solve(table, tile_stiffness, anchor[:, 0])
    nodes = MESH_Y * MESH_X

    def by_tile(field):
        return field.reshape(2, tile_count, nodes).transpose(1, 0, 2)[:, None]

    return match_terms[:, None], by_tile(positions), by_tile(residual)


def solution(mesh):
    return jax.shard_map(
        per_device,
        mesh=mesh,
        in_specs=(
            P("col", "row", None, None, None),
            P("col", "row", None),
            P("col", "row", None),
            P("col", "row"),
            P("col", "row", None),
        ),
        out_specs=(
            P("col", "row", None, None, None),
            P("col", "row", None, None),
            P("col", "row", None, None),
        ),
        check_vma=False,
    )
```
